32 devices in a mesh: pix: 8 (over z, x), peak: 4 (over y, core).
Axes of the slice: x: 2, y: 2, z: 4, core: 2. Of those that a mesh axis runs over, the one named last changes fastest.
Arguments:
- cube: bfloat16 [32768, 8, 2048], P('pix', None, 'peak'), may hold values from -6 to 6
- pix_factor: bfloat16 [32768, 64], P(('pix', 'peak')), may hold values from -0.8984375 to 0.8984375
- sec_factor: bfloat16 [8, 64], replicated, may hold values from -5 to 5
- peak_factor: bfloat16 [2048, 64], P('peak'), may hold values from -0.046875 to 0.046875
Outputs:
- grad_pix: float32 [32768, 64], P(('pix', 'peak'))
- grad_peak: float32 [2048, 64], P('peak')
The draws below stay inside these ranges and needn't reach their ends.
All inputs are finite; a program needn't handle non-finite values.
Results may differ from the reference program's by a relative error of at most 0.0003.
Values may be sent and summed in bfloat16 or wider, within the bound.
A program may use at most 128 MiB of HBM per device.

```python
import math
import jax
import jax.numpy as jnp
from jax import lax

R = 64
PEAKS = 2048
S = 8
PIXELS = 32768


def shard_levels(own_key, dims, cuts, low, largest):
    def one(dim, shards_of):
        steps = jax.random.uniform(jax.random.fold_in(jax.random.fold_in(own_key, 6), dim), (shards_of,), jnp.float32, low / len(cuts), largest / len(cuts))
        return jnp.repeat(jnp.exp(steps), dims[dim] // shards_of).reshape((-1,) + (1,) * (len(dims) - dim - 1))

    gain = one(*cuts[0])
    for cut in cuts[1:]:
        gain = gain * one(*cut)
    return gain


def bell_draw(stream_key, dims, spread, bound, shards=(), kind=jnp.bfloat16):
    array = jax.random.normal(stream_key, dims, jnp.float32) * spread
    if len(shards) > 0:
        array = shard_levels(stream_key, dims, shards, -0.22, 0.18) * array
    return jnp.clip(array, min=-bound, max=bound).astype(kind)


def setup_inputs(seed: int = 0) -> dict:
    key_of = jax.random.split(jax.random.key(seed), 5)
    cube = bell_draw(key_of[0], (PIXELS, S, PEAKS), 1.0, 6.0, ((0, 8), (2, 4)))
    pix_factor = bell_draw(key_of[1], (PIXELS, R), 0.15, 0.8984375, ((0, 32),))
    sec_factor = bell_draw(key_of[2], (S, R), 1.0, 5.0)
    peak_factor = bell_draw(key_of[3], (PEAKS, R), (S * PEAKS) ** -0.5, 0.046875, ((0, 4),))
    return {"cube": cube, "pix_factor": pix_factor, "sec_factor": sec_factor, "peak_factor": peak_factor}


def reference(cube, pix_factor, sec_factor, peak_factor):
    fa = pix_factor.astype(jnp.float32)
    fb = sec_factor.astype(jnp.float32)
    fc = peak_factor.astype(jnp.float32)
    gram_a = jnp.dot(pix_factor.T, pix_factor, preferred_element_type=jnp.float32)
    gram_b = jnp.dot(sec_factor.T, sec_factor, preferred_element_type=jnp.float32)
    gram_c = jnp.dot(peak_factor.T, peak_factor, preferred_element_type=jnp.float32)
    pixels = cube.shape[0]
    sections = cube.shape[1]
    rank = peak_factor.shape[1]
    ttm = jnp.dot(cube.reshape(pixels * sections, cube.shape[2]), peak_factor, preferred_element_type=jnp.float32)
    ttm = ttm.reshape(pixels, sections, rank)
    mttkrp_pix = lax.optimization_barrier(jnp.sum(ttm * fb[None, :, :], axis=1))
    mttkrp_peak = jnp.zeros((cube.shape[2], rank), jnp.float32)
    for index in range(sections):
        inner = jnp.dot(cube[:, index, :].T, pix_factor, preferred_element_type=jnp.float32)
        mttkrp_peak = mttkrp_peak + inner * fb[index][None, :]
    grad_pix = mttkrp_pix - jnp.dot(fa, gram_b * gram_c, precision=lax.Precision.HIGHEST)
    scale = 1.0 / math.sqrt(float(sections * pixels))
    grad_peak = (mttkrp_peak - jnp.dot(fc, gram_a * gram_b, precision=lax.Precision.HIGHEST)) * scale
    return (grad_pix, grad_peak)
```

```python
import functools
import math

import jax
import jax.numpy as jnp
from jax import lax
from jax.experimental import pallas as pl
from jax.experimental.pallas import tpu as pltpu
from jax.sharding import PartitionSpec as P

MESH = pl.DeviceIdType.MESH
F32 = jnp.float32
BF16 = jnp.bfloat16
CHUNK = 256


def dot(a, b):
    return jnp.dot(a, b, preferred_element_type=F32)


def dot_nt(a, b):
    return lax.dot_general(a, b, (((1,), (1,)), ((), ())), preferred_element_type=F32)


def kernel(
    n_pix, n_peak, per_block, scale,
    x_hbm, a_ref, b_ref, c_ref,
    gpix_ref, gpeak_ref,
    xbuf, at, spread, ab, wide, part, sib, far, gc, acc, pbuf, rbuf, cc, bt, ct,
    x_sem, a_ssem, a_rsem, g_ssem, g_rsem, s_ssem, s_rsem, f_ssem, f_rsem,
    r_ssem, r_rsem, o_ssem, o_rsem,
):
    rank = c_ref.shape[1]
    sections = b_ref.shape[0]
    peaks = c_ref.shape[0]
    rows = CHUNK * sections
    half = CHUNK // 2
    n_chip = n_peak // 2
    wide_r = 2 * rank
    pix = lax.axis_index("pix")
    me = lax.axis_index("peak")
    chip = me // 2
    core = lax.rem(me, 2)
    sibling = 2 * chip + 1 - core

    blocks = []
    for d in range(1, n_chip):
        other = lax.rem(chip + d, n_chip)
        blocks += [2 * other + 1 - core, 2 * other + core]
    blocks += [sibling, me]

    def x_copy(pos, k):
        first = (blocks[pos] * per_block + k) * rows
        return pltpu.make_async_copy(
            x_hbm.at[pl.ds(pl.multiple_of(first, rows), rows), :],
            xbuf.at[pos * per_block + k],
            x_sem.at[pos * per_block + k],
        )

    for pos in range(n_peak):
        for k in range(per_block):
            x_copy(pos, k).start()

    barrier = pltpu.get_barrier_semaphore()
    for d in range(1, n_peak):
        pl.semaphore_signal(
            barrier, inc=1, device_id=(pix, lax.rem(me + d, n_peak)), device_id_type=MESH
        )
    for d in range(1, n_pix):
        pl.semaphore_signal(
            barrier, inc=1, device_id=(lax.rem(pix + d, n_pix), me), device_id_type=MESH
        )

    row = lax.broadcasted_iota(jnp.int32, (rank, rank), 0)
    col = lax.broadcasted_iota(jnp.int32, (rank, rank), 1)
    eye = (row == col).astype(F32).astype(BF16)
    row = lax.broadcasted_iota(jnp.int32, (rank, wide_r), 0)
    col = lax.broadcasted_iota(jnp.int32, (rank, wide_r), 1)
    eye2 = ((row == col) | (row + rank == col)).astype(F32).astype(BF16)
    own = n_peak - 1
    for k in range(per_block):
        at[own, k] = dot_nt(eye, a_ref[k * CHUNK:(k + 1) * CHUNK, :]).astype(BF16)
    ct[...] = dot_nt(eye, c_ref[...]).astype(BF16)
    cc[...] = dot(c_ref[...], eye2).astype(BF16)
    gc[0] = dot(ct[...], cc[...])
    b_f = b_ref[...].astype(F32)
    b_tiled = jnp.broadcast_to(b_f[None], (CHUNK // sections, sections, rank))
    b_tiled = b_tiled.reshape(CHUNK, rank)
    bt[...] = dot_nt(eye, b_tiled.astype(BF16))
    bb = dot(b_ref[...], eye2)
    lead = lax.broadcasted_iota(jnp.int32, (CHUNK, rank), 0) < sections
    b_once = jnp.where(lead, b_tiled, 0.0).astype(BF16)
    gram_b2 = dot(dot_nt(eye, b_once).astype(BF16), dot(b_once, eye2).astype(BF16))
    row = lax.broadcasted_iota(jnp.int32, (CHUNK, CHUNK), 0)
    col = lax.broadcasted_iota(jnp.int32, (CHUNK, CHUNK), 1) // sections
    for j in range(sections):
        spread[j] = (row == col + j * (CHUNK // sections)).astype(F32).astype(BF16)

    pl.semaphore_wait(barrier, n_peak - 1 + n_pix - 1)

    def a_send(index, src, dst, device):
        return pltpu.make_async_remote_copy(
            src_ref=at.at[src], dst_ref=at.at[dst],
            send_sem=a_ssem.at[index], recv_sem=a_rsem.at[dst],
            device_id=(pix, device), device_id_type=MESH,
        )

    a_out = []
    for d in range(1, n_chip):
        device = 2 * lax.rem(chip - d + n_chip, n_chip) + core
        a_out.append(a_send(2 * (d - 1), own, 2 * (d - 1) + 1, device))
        a_out[-1].start()
    a_out.append(a_send(n_peak - 2, own, n_peak - 2, sibling))
    a_out[-1].start()
    a_fwd = [
        a_send(2 * (d - 1) + 1, 2 * (d - 1) + 1, 2 * (d - 1), sibling) for d in range(1, n_chip)
    ]

    g_out = []
    for d in range(1, n_peak):
        g_out.append(pltpu.make_async_remote_copy(
            src_ref=gc.at[0], dst_ref=gc.at[d],
            send_sem=g_ssem.at[d - 1], recv_sem=g_rsem.at[d - 1],
            device_id=(pix, lax.rem(me + d, n_peak)), device_id_type=MESH,
        ))
        g_out[-1].start()

    lane_lo = lax.broadcasted_iota(jnp.int32, (half * sections, wide_r), 1) < rank
    lane_lo_half = lax.broadcasted_iota(jnp.int32, (half, wide_r), 1) < rank

    def pix_mode(pos, wait):
        def body(k, carry):
            if wait:
                x_copy(pos, k).wait()
            at_k = pos * per_block + k
            one = dot(xbuf[at_k, : half * sections, :], cc[...])
            two = dot(xbuf[at_k, half * sections:, :], cc[...])
            wide[...] = jnp.where(lane_lo, one, two)
            total = wide[pl.ds(0, half, stride=sections), :] * bb[0:1, :]
            for s in range(1, sections):
                total += wide[pl.ds(s, half, stride=sections), :] * bb[s:s + 1, :]
            part[pos, k] = total
            return carry

        lax.fori_loop(0, per_block, body, 0)

    def peak_mode(pos, wait):
        def body(k, carry):
            if wait:
                x_copy(pos, k).wait()
            for j in range(sections):
                product = dot(at[pos, k], spread[j]) * bt[...]
                high = product.astype(BF16)
                ab[:rank, j * CHUNK:(j + 1) * CHUNK] = high
                ab[rank:, j * CHUNK:(j + 1) * CHUNK] = (product - high.astype(F32)).astype(BF16)
            acc[...] += dot(ab[...], xbuf[pos * per_block + k])
            return carry

        lax.fori_loop(0, per_block, body, 0)

    def sib_send(pos):
        return pltpu.make_async_remote_copy(
            src_ref=part.at[pos], dst_ref=sib.at[pos // 2],
            send_sem=s_ssem.at[pos // 2], recv_sem=s_rsem.at[pos // 2],
            device_id=(pix, sibling), device_id_type=MESH,
        )

    def far_send(d):
        device = 2 * lax.rem(chip + d, n_chip) + core
        return pltpu.make_async_remote_copy(
            src_ref=part.at[2 * (d - 1) + 1], dst_ref=far.at[d - 1],
            send_sem=f_ssem.at[d - 1], recv_sem=f_rsem.at[d - 1],
            device_id=(pix, device), device_id_type=MESH,
        )

    acc[...] = jnp.zeros_like(acc)
    for d in range(1, n_chip):
        pix_mode(2 * (d - 1), True)
        sib_send(2 * (d - 1)).start()
        pix_mode(2 * (d - 1) + 1, True)
        sib_send(2 * (d - 1)).wait_recv()
        part[2 * (d - 1) + 1] += sib[d - 1]
        far_send(d).start()
        a_out[d - 1].wait_recv()
        a_fwd[d - 1].start()

    peak_mode(n_peak - 1, True)
    a_out[-1].wait_recv()
    peak_mode(n_peak - 2, True)
    for d in range(1, n_chip):
        peak_mode(2 * (d - 1) + 1, False)
        a_fwd[d - 1].wait_recv()
        peak_mode(2 * (d - 1), False)

    gram_a = jnp.zeros((rank, rank), F32)
    for pos in range(n_peak):
        for k in range(per_block):
            gram_a += dot_nt(at[pos, k], at[pos, k])
    corr = jnp.dot(
        gram_a * gram_b2[:, :rank], ct[...].astype(F32),
        precision=lax.Precision.HIGHEST, preferred_element_type=F32,
    )
    partial = (acc[:rank, :] + acc[rank:, :] - corr) * scale
    pbuf[...] = partial.reshape(pbuf.shape)

    r_out = []
    for d in range(1, n_pix):
        device = lax.rem(pix + d, n_pix)
        r_out.append(pltpu.make_async_remote_copy(
            src_ref=pbuf.at[device], dst_ref=rbuf.at[d - 1],
            send_sem=r_ssem.at[d - 1], recv_sem=r_rsem.at[d - 1],
            device_id=(device, me), device_id_type=MESH,
        ))
        r_out[-1].start()

    pix_mode(n_peak - 2, False)
    sib_send(n_peak - 2).start()

    for d in range(1, n_pix):
        r_out[d - 1].wait_recv()
    total = pbuf[pix]
    for d in range(1, n_pix):
        total += rbuf[d - 1]
    gpeak_ref[pix] = total
    o_out = []
    for d in range(1, n_pix):
        device = lax.rem(pix + d, n_pix)
        o_out.append(pltpu.make_async_remote_copy(
            src_ref=gpeak_ref.at[pix], dst_ref=gpeak_ref.at[pix],
            send_sem=o_ssem.at[d - 1], recv_sem=o_rsem.at[d - 1],
            device_id=(device, me), device_id_type=MESH,
        ))
        o_out[-1].start()

    pix_mode(n_peak - 1, False)

    for d in range(1, n_peak):
        g_out[d - 1].wait_recv()
    gram_c = gc[0]
    for d in range(1, n_peak):
        gram_c += gc[d]
    weight = gram_b2 * gram_c
    w1 = weight.astype(BF16)
    rest = weight - w1.astype(F32)
    w2 = rest.astype(BF16)
    w3 = (rest - w2.astype(F32)).astype(BF16)

    for d in range(1, n_chip):
        far_send(d).wait_recv()
    sib_send(n_peak - 2).wait_recv()
    for k in range(per_block):
        a_k = a_ref[k * CHUNK:(k + 1) * CHUNK, :]
        both = dot(a_k, w1) + (dot(a_k, w2) + dot(a_k, w3))
        total = part[own, k] + sib[n_chip - 1, k]
        for d in range(1, n_chip):
            total += far[d - 1, k]
        total -= jnp.where(lane_lo_half, both[:half], both[half:])
        gpix_ref[k * CHUNK:k * CHUNK + half, :] = total[:, :rank]
        gpix_ref[k * CHUNK + half:(k + 1) * CHUNK, :] = total[:, rank:]

    for d in range(1, n_pix):
        o_out[d - 1].wait_recv()
    for copy in a_out + a_fwd + g_out + r_out + o_out:
        copy.wait_send()
    for pos in range(0, n_peak, 2):
        sib_send(pos).wait_send()
    for d in range(1, n_chip):
        far_send(d).wait_send()


def solution(mesh):
    n_pix, n_peak = mesh.shape["pix"], mesh.shape["peak"]

    def on_device(cube, pix_factor, sec_factor, peak_factor):
        pixels, sections, peaks = cube.shape
        rank = peak_factor.shape[1]
        own = pix_factor.shape[0]
        per_block = own // CHUNK
        rows = CHUNK * sections
        n_chip = n_peak // 2
        scale = 1.0 / math.sqrt(float(sections * pixels * n_pix))
        dma = pltpu.SemaphoreType.DMA
        vmem = pl.BlockSpec(memory_space=pltpu.VMEM)
        grad_pix, grad_peak = pl.pallas_call(
            functools.partial(kernel, n_pix, n_peak, per_block, scale),
            out_shape=(
                jax.ShapeDtypeStruct((own, rank), F32),
                jax.ShapeDtypeStruct((n_pix, rank // n_pix, peaks), F32),
            ),
            in_specs=[pl.BlockSpec(memory_space=pl.ANY), vmem, vmem, vmem],
            out_specs=(vmem, vmem),
            scratch_shapes=[
                pltpu.VMEM((n_peak * per_block, rows, peaks), BF16),
                pltpu.VMEM((n_peak, per_block, rank, CHUNK), BF16),
                pltpu.VMEM((sections, CHUNK, CHUNK), BF16),
                pltpu.VMEM((2 * rank, rows), BF16),
                pltpu.VMEM((rows // 2, 2 * rank), F32),
                pltpu.VMEM((n_peak, per_block, CHUNK // 2, 2 * rank), F32),
                pltpu.VMEM((n_chip, per_block, CHUNK // 2, 2 * rank), F32),
                pltpu.VMEM((max(n_chip - 1, 1), per_block, CHUNK // 2, 2 * rank), F32),
                pltpu.VMEM((n_peak, rank, 2 * rank), F32),
                pltpu.VMEM((2 * rank, peaks), F32),
                pltpu.VMEM((n_pix, rank // n_pix, peaks), F32),
                pltpu.VMEM((n_pix - 1, rank // n_pix, peaks), F32),
                pltpu.VMEM((peaks, 2 * rank), BF16),
                pltpu.VMEM((rank, CHUNK), F32),
                pltpu.VMEM((rank, peaks), BF16),
                dma((n_peak * per_block,)),
                dma((n_peak - 1,)), dma((n_peak - 1,)),
                dma((n_peak - 1,)), dma((n_peak - 1,)),
                dma((n_chip,)), dma((n_chip,)),
                dma((max(n_chip - 1, 1),)), dma((max(n_chip - 1, 1),)),
                dma((n_pix - 1,)), dma((n_pix - 1,)),
                dma((n_pix - 1,)), dma((n_pix - 1,)),
            ],
            compiler_params=pltpu.CompilerParams(
                collective_id=0, has_side_effects=True, vmem_limit_bytes=56 * 1024 * 1024
            ),
            name="cp_gradient",
        )(cube.reshape(pixels * sections, peaks), pix_factor, sec_factor, peak_factor)
        return grad_pix, grad_peak.reshape(rank, peaks).T

    in_specs = (P("pix", None, "peak"), P(("pix", "peak"), None), P(), P("peak", None))
    out_specs = (P(("pix", "peak"), None), P("peak", None))
    return jax.shard_map(
        on_device, mesh=mesh, in_specs=in_specs, out_specs=out_specs, check_vma=False
    )
```

```python
import functools
import math

import jax
import jax.numpy as jnp
from jax import lax
from jax.experimental import pallas as pl
from jax.experimental.pallas import tpu as pltpu
from jax.sharding import PartitionSpec as P

MESH = pl.DeviceIdType.MESH
F32 = jnp.float32
BF16 = jnp.bfloat16
CHUNK = 256


def dot(a, b):
    return jnp.dot(a, b, preferred_element_type=F32)


def dot_nt(a, b):
    return lax.dot_general(a, b, (((1,), (1,)), ((), ())), preferred_element_type=F32)


def split3(x):
    one = x.astype(BF16)
    rest = x - one.astype(F32)
    two = rest.astype(BF16)
    return one, two, (rest - two.astype(F32)).astype(BF16)


def dot3(parts, b):
    return dot(parts[0], b) + (dot(parts[1], b) + dot(parts[2], b))


def kernel(
    n_pix, n_peak, per_block, scale,
    x_hbm, a_ref, b_ref, c_ref,
    gpix_ref, gpeak_ref,
    xbuf, at, spread, ab, wide, part, sib, far, gc, acc, pbuf, rbuf, cc, bt, ga, fix,
    x_sem, a_ssem, a_rsem, g_ssem, g_rsem, s_ssem, s_rsem, f_ssem, f_rsem,
    r_ssem, r_rsem, o_ssem, o_rsem,
):
    rank = c_ref.shape[0]
    sections = b_ref.shape[0]
    rows = CHUNK * sections
    half = CHUNK // 2
    n_chip = n_peak // 2
    wide_r = 2 * rank
    pix = lax.axis_index("pix")
    me = lax.axis_index("peak")
    chip = me // 2
    core = lax.rem(me, 2)
    sibling = 2 * chip + 1 - core
    own = n_peak - 1
    near = n_peak - 2

    blocks = []
    for d in range(1, n_chip):
        other = lax.rem(chip + d, n_chip)
        blocks += [2 * other + 1 - core, 2 * other + core]
    blocks += [sibling, me]

    pairs = [(d, k) for k in range(per_block) for d in range(1, n_chip)]
    early = pairs[:len(pairs) // 4], pairs[len(pairs) // 4:len(pairs) // 2]
    late = pairs[len(pairs) // 2:]

    def x_copy(pos, k):
        first = (blocks[pos] * per_block + k) * rows
        return pltpu.make_async_copy(
            x_hbm.at[pl.ds(pl.multiple_of(first, rows), rows), :],
            xbuf.at[pos * per_block + k],
            x_sem.at[pos * per_block + k],
        )

    def pair_x(d, k):
        return [x_copy(2 * (d - 1), k), x_copy(2 * (d - 1) + 1, k)]

    order = [c for p in early[0] for c in pair_x(*p)] + [x_copy(own, k) for k in range(per_block)]
    order += [c for p in early[1] for c in pair_x(*p)] + [x_copy(near, k) for k in range(per_block)]
    order += [c for p in late for c in pair_x(*p)]
    for copy in order:
        copy.start()

    barrier = pltpu.get_barrier_semaphore()
    for d in range(1, n_peak):
        pl.semaphore_signal(
            barrier, inc=1, device_id=(pix, lax.rem(me + d, n_peak)), device_id_type=MESH
        )
    for d in range(1, n_pix):
        pl.semaphore_signal(
            barrier, inc=1, device_id=(lax.rem(pix + d, n_pix), me), device_id_type=MESH
        )

    for k in range(per_block):
        at[own, k] = a_ref[:, k * CHUNK:(k + 1) * CHUNK]
    ct = c_ref[...].astype(F32)
    cc[...] = jnp.concatenate([ct, ct], axis=0).T.astype(BF16)
    gc[0] = dot(c_ref[...], cc[...])

    pl.semaphore_wait(barrier, n_peak - 1 + n_pix - 1)

    def a_send(index, src, dst, device):
        return pltpu.make_async_remote_copy(
            src_ref=at.at[src], dst_ref=at.at[dst],
            send_sem=a_ssem.at[index], recv_sem=a_rsem.at[dst],
            device_id=(pix, device), device_id_type=MESH,
        )

    a_out = []
    for d in range(1, n_chip):
        device = 2 * lax.rem(chip - d + n_chip, n_chip) + core
        a_out.append(a_send(2 * (d - 1), own, 2 * (d - 1) + 1, device))
        a_out[-1].start()
    a_out.append(a_send(near, own, near, sibling))
    a_out[-1].start()
    a_fwd = [
        a_send(2 * (d - 1) + 1, 2 * (d - 1) + 1, 2 * (d - 1), sibling) for d in range(1, n_chip)
    ]

    g_out = []
    for d in range(1, n_peak):
        g_out.append(pltpu.make_async_remote_copy(
            src_ref=gc.at[0], dst_ref=gc.at[d],
            send_sem=g_ssem.at[d - 1], recv_sem=g_rsem.at[d - 1],
            device_id=(pix, lax.rem(me + d, n_peak)), device_id_type=MESH,
        ))
        g_out[-1].start()

    row = lax.broadcasted_iota(jnp.int32, (rank, rank), 0)
    col = lax.broadcasted_iota(jnp.int32, (rank, rank), 1)
    eye = (row == col).astype(F32).astype(BF16)
    row = lax.broadcasted_iota(jnp.int32, (rank, wide_r), 0)
    col = lax.broadcasted_iota(jnp.int32, (rank, wide_r), 1)
    eye2 = ((row == col) | (row + rank == col)).astype(F32).astype(BF16)
    b_f = b_ref[...].astype(F32)
    b_tiled = jnp.broadcast_to(b_f[None], (CHUNK // sections, sections, rank))
    b_tiled = b_tiled.reshape(CHUNK, rank)
    bt[...] = dot_nt(eye, b_tiled.astype(BF16))
    bb = dot(b_ref[...], eye2)
    lead = lax.broadcasted_iota(jnp.int32, (CHUNK, rank), 0) < sections
    b_once = jnp.where(lead, b_tiled, 0.0).astype(BF16)
    gram_b = dot(dot_nt(eye, b_once).astype(BF16), b_once)
    row = lax.broadcasted_iota(jnp.int32, (CHUNK, CHUNK), 0)
    col = lax.broadcasted_iota(jnp.int32, (CHUNK, CHUNK), 1) // sections
    for j in range(sections):
        spread[j] = (row == col + j * (CHUNK // sections)).astype(F32).astype(BF16)
    ga[...] = jnp.zeros_like(ga)

    lane_lo = lax.broadcasted_iota(jnp.int32, (half * sections, wide_r), 1) < rank

    def pix_chunks(todo):
        for index, slot in todo:
            one = dot(xbuf[index, : half * sections, :], cc[...])
            two = dot(xbuf[index, half * sections:, :], cc[...])
            wide[slot] = jnp.where(lane_lo, one, two)
        for index, slot in todo:
            total = wide[slot, pl.ds(0, half, stride=sections), :] * bb[0:1, :]
            for s in range(1, sections):
                total += wide[slot, pl.ds(s, half, stride=sections), :] * bb[s:s + 1, :]
            part[index] = total

    def expand(pos):
        stacked = at[pos].reshape(per_block * rank, CHUNK)
        for j in range(sections):
            product = dot(stacked, spread[j]).reshape(per_block, rank, CHUNK) * bt[...][None]
            high = product.astype(BF16)
            low = (product - high.astype(F32)).astype(BF16)
            first = pos * per_block
            ab[first:first + per_block, :rank, j * CHUNK:(j + 1) * CHUNK] = high
            ab[first:first + per_block, rank:, j * CHUNK:(j + 1) * CHUNK] = low
        for k in range(per_block):
            ga[...] += dot_nt(at[pos, k], at[pos, k])

    def peak_mode(first, count, copy):
        step = 2 if count % 2 == 0 else 1

        def body(i, carry):
            if copy is not None:
                for k in range(step):
                    copy(i * step + k).wait()
            total = acc[...]
            for k in range(step):
                index = first + i * step + k
                total += dot(ab[index], xbuf[index])
            acc[...] = total
            return carry

        lax.fori_loop(0, count // step, body, 0)

    def sib_send(chip_slot, k):
        pos = 2 * chip_slot
        return pltpu.make_async_remote_copy(
            src_ref=part.at[pos * per_block + k], dst_ref=sib.at[chip_slot, k],
            send_sem=s_ssem.at[chip_slot, k], recv_sem=s_rsem.at[chip_slot, k],
            device_id=(pix, sibling), device_id_type=MESH,
        )

    def far_send(d, k):
        device = 2 * lax.rem(chip + d, n_chip) + core
        pos = 2 * (d - 1) + 1
        return pltpu.make_async_remote_copy(
            src_ref=part.at[pos * per_block + k], dst_ref=far.at[d - 1, k],
            send_sem=f_ssem.at[d - 1, k], recv_sem=f_rsem.at[d - 1, k],
            device_id=(pix, device), device_id_type=MESH,
        )

    def pair_mode(d, k):
        index = 2 * (d - 1) * per_block + k
        pix_chunks([(index, 0), (index + per_block, 1)])
        sib_send(d - 1, k).start()

    def pair_finish(d, k):
        sib_send(d - 1, k).wait_recv()
        part[(2 * (d - 1) + 1) * per_block + k] += sib[d - 1, k]
        far_send(d, k).start()

    acc[...] = jnp.zeros_like(acc)
    expand(own)
    for p in early[0]:
        for copy in pair_x(*p):
            copy.wait()
        pair_mode(*p)
    peak_mode(own * per_block, per_block, lambda k: x_copy(own, k))
    for p in early[0]:
        pair_finish(*p)
    a_out[-1].wait_recv()
    for p in early[1]:
        for copy in pair_x(*p):
            copy.wait()
    expand(near)
    for p in early[1]:
        pair_mode(*p)
    for d in range(1, n_chip):
        a_out[d - 1].wait_recv()
        a_fwd[d - 1].start()
    peak_mode(near * per_block, per_block, lambda k: x_copy(near, k))
    for p in early[1]:
        pair_finish(*p)
    for d in range(1, n_chip):
        a_fwd[d - 1].wait_recv()
    for pos in range(near):
        expand(pos)
    acc[:rank, :] -= dot3(split3(ga[...] * gram_b), c_ref[...])
    for p in late:
        for copy in pair_x(*p):
            copy.wait()
    peak_mode(0, near * per_block, None)

    pbuf[...] = ((acc[:rank, :] + acc[rank:, :]) * scale).reshape(pbuf.shape)
    r_out = []
    for d in range(1, n_pix):
        device = lax.rem(pix + d, n_pix)
        r_out.append(pltpu.make_async_remote_copy(
            src_ref=pbuf.at[device], dst_ref=rbuf.at[d - 1],
            send_sem=r_ssem.at[d - 1], recv_sem=r_rsem.at[d - 1],
            device_id=(device, me), device_id_type=MESH,
        ))
        r_out[-1].start()

    for n, p in enumerate(late):
        pair_mode(*p)
        if n > 0:
            pair_finish(*late[n - 1])

    def single_mode(pos, send):
        step = 2 if per_block % 2 == 0 else 1

        def body(i, carry):
            first = pos * per_block + i * step
            pix_chunks([(first + k, k) for k in range(step)])
            if send:
                for k in range(step):
                    sib_send(n_chip - 1, i * step + k).start()
            return carry

        lax.fori_loop(0, per_block // step, body, 0)

    for d in range(1, n_peak):
        g_out[d - 1].wait_recv()
    gram_c = gc[0]
    for d in range(1, n_peak):
        gram_c += gc[d]
    weight = split3(gram_b * gram_c[:, :rank])
    for k in range(per_block):
        fix[k] = dot3(weight, at[own, k])
    single_mode(near, True)
    for p in late[-1:]:
        pair_finish(*p)

    for d in range(1, n_pix):
        r_out[d - 1].wait_recv()
    total = pbuf[pix]
    for d in range(1, n_pix):
        total += rbuf[d - 1]
    gpeak_ref[pix] = total
    o_out = []
    for d in range(1, n_pix):
        device = lax.rem(pix + d, n_pix)
        o_out.append(pltpu.make_async_remote_copy(
            src_ref=gpeak_ref.at[pix], dst_ref=gpeak_ref.at[pix],
            send_sem=o_ssem.at[d - 1], recv_sem=o_rsem.at[d - 1],
            device_id=(device, me), device_id_type=MESH,
        ))
        o_out[-1].start()

    single_mode(own, False)

    for k in range(per_block):
        sib_send(n_chip - 1, k).wait_recv()
    for p in pairs:
        far_send(*p).wait_recv()
    for k in range(per_block):
        total = part[own * per_block + k] + sib[n_chip - 1, k]
        for d in range(1, n_chip):
            total += far[d - 1, k]
        total = total.T
        lo = k * CHUNK
        gpix_ref[:, lo:lo + half] = total[:rank] - fix[k, :, :half]
        gpix_ref[:, lo + half:lo + CHUNK] = total[rank:] - fix[k, :, half:]

    for d in range(1, n_pix):
        o_out[d - 1].wait_recv()
    for copy in a_out + a_fwd + g_out + r_out + o_out:
        copy.wait_send()
    for chip_slot in range(n_chip):
        for k in range(per_block):
            sib_send(chip_slot, k).wait_send()
    for p in pairs:
        far_send(*p).wait_send()


def place(pix_in, peak_in, pix_out, peak_out, sem):
    copies = [
        pltpu.make_async_copy(pix_in, pix_out, sem.at[0]),
        pltpu.make_async_copy(peak_in, peak_out, sem.at[1]),
    ]
    for copy in copies:
        copy.start()
    for copy in copies:
        copy.wait()


def solution(mesh):
    n_pix, n_peak = mesh.shape["pix"], mesh.shape["peak"]

    def on_device(cube, pix_factor, sec_factor, peak_factor):
        pixels, sections, peaks = cube.shape
        rank = peak_factor.shape[1]
        own = pix_factor.shape[0]
        per_block = own // CHUNK
        rows = CHUNK * sections
        n_chip = n_peak // 2
        n_far = max(n_chip - 1, 1)
        n_chunk = n_peak * per_block
        scale = 1.0 / math.sqrt(float(sections * pixels * n_pix))
        dma = pltpu.SemaphoreType.DMA
        vmem = pl.BlockSpec(memory_space=pltpu.VMEM)
        anywhere = pl.BlockSpec(memory_space=pl.ANY)
        packed = (CHUNK // 2, 2 * rank)
        grad_pix, grad_peak = pl.pallas_call(
            functools.partial(kernel, n_pix, n_peak, per_block, scale),
            out_shape=(
                jax.ShapeDtypeStruct((rank, own), F32),
                jax.ShapeDtypeStruct((n_pix, rank // n_pix, peaks), F32),
            ),
            in_specs=[anywhere, vmem, vmem, vmem],
            out_specs=(vmem, vmem),
            scratch_shapes=[
                pltpu.VMEM((n_chunk, rows, peaks), BF16),
                pltpu.VMEM((n_peak, per_block, rank, CHUNK), BF16),
                pltpu.VMEM((sections, CHUNK, CHUNK), BF16),
                pltpu.VMEM((n_chunk, 2 * rank, rows), BF16),
                pltpu.VMEM((2, rows // 2, 2 * rank), F32),
                pltpu.VMEM((n_chunk,) + packed, F32),
                pltpu.VMEM((n_chip, per_block) + packed, F32),
                pltpu.VMEM((n_far, per_block) + packed, F32),
                pltpu.VMEM((n_peak, rank, 2 * rank), F32),
                pltpu.VMEM((2 * rank, peaks), F32),
                pltpu.VMEM((n_pix, rank // n_pix, peaks), F32),
                pltpu.VMEM((n_pix - 1, rank // n_pix, peaks), F32),
                pltpu.VMEM((peaks, 2 * rank), BF16),
                pltpu.VMEM((rank, CHUNK), F32),
                pltpu.VMEM((rank, rank), F32),
                pltpu.VMEM((per_block, rank, CHUNK), F32),
                dma((n_chunk,)),
                dma((n_peak - 1,)), dma((n_peak - 1,)),
                dma((n_peak - 1,)), dma((n_peak - 1,)),
                dma((n_chip, per_block)), dma((n_chip, per_block)),
                dma((n_far, per_block)), dma((n_far, per_block)),
                dma((n_pix - 1,)), dma((n_pix - 1,)),
                dma((n_pix - 1,)), dma((n_pix - 1,)),
            ],
            compiler_params=pltpu.CompilerParams(
                collective_id=0, has_side_effects=True, vmem_limit_bytes=56 * 1024 * 1024
            ),
            name="cp_gradient",
        )(cube.reshape(pixels * sections, peaks), pix_factor.T, sec_factor, peak_factor.T)
        grad_pix, grad_peak = pl.pallas_call(
            place,
            out_shape=(
                jax.ShapeDtypeStruct((rank, own), F32),
                jax.ShapeDtypeStruct((rank, peaks), F32),
            ),
            in_specs=[pl.BlockSpec(memory_space=pltpu.HBM)] * 2,
            out_specs=(anywhere, anywhere),
            scratch_shapes=[dma((2,))],
            name="place_results",
        )(grad_pix, grad_peak.reshape(rank, peaks))
        return grad_pix.T, grad_peak.T

    in_specs = (P("pix", None, "peak"), P(("pix", "peak"), None), P(), P("peak", None))
    out_specs = (P(("pix", "peak"), None), P("peak", None))
    return jax.shard_map(
        on_device, mesh=mesh, in_specs=in_specs, out_specs=out_specs, check_vma=False
    )
```

```python
import functools
import math

import jax
import jax.numpy as jnp
from jax import lax
from jax.experimental import pallas as pl
from jax.experimental.pallas import tpu as pltpu
from jax.sharding import PartitionSpec as P

MESH = pl.DeviceIdType.MESH
F32 = jnp.float32
BF16 = jnp.bfloat16
CHUNK = 256


def dot(a, b):
    return jnp.dot(a, b, preferred_element_type=F32)


def dot_nt(a, b):
    return lax.dot_general(a, b, (((1,), (1,)), ((), ())), preferred_element_type=F32)


def split3(x):
    one = x.astype(BF16)
    rest = x - one.astype(F32)
    two = rest.astype(BF16)
    return one, two, (rest - two.astype(F32)).astype(BF16)


def dot3(parts, b):
    return dot(parts[0], b) + (dot(parts[1], b) + dot(parts[2], b))


def kernel(
    n_pix, n_peak, per_block, scale,
    x_hbm, a_ref, b_ref, c_ref,
    gpix_ref, gpeak_ref,
    xbuf, at, spread, ab, wide, part, sib, far, gc, acc, pbuf, rbuf, cc, bt, ga, fix,
    x_sem, a_ssem, a_rsem, g_ssem, g_rsem, s_ssem, s_rsem, f_ssem, f_rsem,
    r_ssem, r_rsem, o_ssem, o_rsem,
):
    rank = c_ref.shape[0]
    sections = b_ref.shape[0]
    rows = CHUNK * sections
    half = CHUNK // 2
    n_chip = n_peak // 2
    wide_r = 2 * rank
    pix = lax.axis_index("pix")
    me = lax.axis_index("peak")
    chip = me // 2
    core = lax.rem(me, 2)
    sibling = 2 * chip + 1 - core
    own = n_peak - 1
    near = n_peak - 2

    blocks = []
    for d in range(1, n_chip):
        other = lax.rem(chip + d, n_chip)
        blocks += [2 * other + 1 - core, 2 * other + core]
    blocks += [sibling, me]

    pairs = [(d, k) for k in range(per_block) for d in range(1, n_chip)]
    cuts = [len(pairs) * n // 4 for n in range(5)]
    first, second, third, late = [pairs[lo:hi] for lo, hi in zip(cuts, cuts[1:])]

    def x_copy(pos, k):
        first = (blocks[pos] * per_block + k) * rows
        return pltpu.make_async_copy(
            x_hbm.at[pl.ds(pl.multiple_of(first, rows), rows), :],
            xbuf.at[pos * per_block + k],
            x_sem.at[pos * per_block + k],
        )

    def pair_x(d, k):
        return [x_copy(2 * (d - 1), k), x_copy(2 * (d - 1) + 1, k)]

    order = [c for p in first for c in pair_x(*p)] + [x_copy(own, k) for k in range(per_block)]
    order += [c for p in second for c in pair_x(*p)] + [x_copy(near, k) for k in range(per_block)]
    order += [c for p in third + late for c in pair_x(*p)]
    for copy in order:
        copy.start()

    barrier = pltpu.get_barrier_semaphore()
    for d in range(1, n_peak):
        pl.semaphore_signal(
            barrier, inc=1, device_id=(pix, lax.rem(me + d, n_peak)), device_id_type=MESH
        )
    for d in range(1, n_pix):
        pl.semaphore_signal(
            barrier, inc=1, device_id=(lax.rem(pix + d, n_pix), me), device_id_type=MESH
        )

    for k in range(per_block):
        at[own, k] = a_ref[:, k * CHUNK:(k + 1) * CHUNK]
    ct = c_ref[...].astype(F32)
    cc[...] = jnp.concatenate([ct, ct], axis=0).T.astype(BF16)
    gc[0] = dot(c_ref[...], cc[...])

    pl.semaphore_wait(barrier, n_peak - 1 + n_pix - 1)

    def a_send(index, src, dst, device):
        return pltpu.make_async_remote_copy(
            src_ref=at.at[src], dst_ref=at.at[dst],
            send_sem=a_ssem.at[index], recv_sem=a_rsem.at[dst],
            device_id=(pix, device), device_id_type=MESH,
        )

    a_out = []
    for d in range(1, n_chip):
        device = 2 * lax.rem(chip - d + n_chip, n_chip) + core
        a_out.append(a_send(2 * (d - 1), own, 2 * (d - 1) + 1, device))
        a_out[-1].start()
    a_out.append(a_send(near, own, near, sibling))
    a_out[-1].start()
    a_fwd = [
        a_send(2 * (d - 1) + 1, 2 * (d - 1) + 1, 2 * (d - 1), sibling) for d in range(1, n_chip)
    ]

    g_out = []
    for d in range(1, n_peak):
        g_out.append(pltpu.make_async_remote_copy(
            src_ref=gc.at[0], dst_ref=gc.at[d],
            send_sem=g_ssem.at[d - 1], recv_sem=g_rsem.at[d - 1],
            device_id=(pix, lax.rem(me + d, n_peak)), device_id_type=MESH,
        ))
        g_out[-1].start()

    row = lax.broadcasted_iota(jnp.int32, (rank, rank), 0)
    col = lax.broadcasted_iota(jnp.int32, (rank, rank), 1)
    eye = (row == col).astype(F32).astype(BF16)
    row = lax.broadcasted_iota(jnp.int32, (rank, wide_r), 0)
    col = lax.broadcasted_iota(jnp.int32, (rank, wide_r), 1)
    eye2 = ((row == col) | (row + rank == col)).astype(F32).astype(BF16)
    b_f = b_ref[...].astype(F32)
    b_tiled = jnp.broadcast_to(b_f[None], (CHUNK // sections, sections, rank))
    b_tiled = b_tiled.reshape(CHUNK, rank)
    bt[...] = dot_nt(eye, b_tiled.astype(BF16))
    bb = dot(b_ref[...], eye2)
    lead = lax.broadcasted_iota(jnp.int32, (CHUNK, rank), 0) < sections
    b_once = jnp.where(lead, b_tiled, 0.0).astype(BF16)
    gram_b = dot(dot_nt(eye, b_once).astype(BF16), b_once)
    row = lax.broadcasted_iota(jnp.int32, (CHUNK, CHUNK), 0)
    col = lax.broadcasted_iota(jnp.int32, (CHUNK, CHUNK), 1) // sections
    for j in range(sections):
        spread[j] = (row == col + j * (CHUNK // sections)).astype(F32).astype(BF16)
    ga[...] = jnp.zeros_like(ga)

    lane_lo = lax.broadcasted_iota(jnp.int32, (half * sections, wide_r), 1) < rank

    def pix_chunks(todo):
        for index, slot in todo:
            one = dot(xbuf[index, : half * sections, :], cc[...])
            two = dot(xbuf[index, half * sections:, :], cc[...])
            wide[slot] = jnp.where(lane_lo, one, two)
        for index, slot in todo:
            total = wide[slot, pl.ds(0, half, stride=sections), :] * bb[0:1, :]
            for s in range(1, sections):
                total += wide[slot, pl.ds(s, half, stride=sections), :] * bb[s:s + 1, :]
            part[index] = total

    def expand(pos):
        stacked = at[pos].reshape(per_block * rank, CHUNK)
        for j in range(sections):
            product = dot(stacked, spread[j]).reshape(per_block, rank, CHUNK) * bt[...][None]
            high = product.astype(BF16)
            low = (product - high.astype(F32)).astype(BF16)
            first = pos * per_block
            ab[first:first + per_block, :rank, j * CHUNK:(j + 1) * CHUNK] = high
            ab[first:first + per_block, rank:, j * CHUNK:(j + 1) * CHUNK] = low
        for k in range(per_block):
            ga[...] += dot_nt(at[pos, k], at[pos, k])

    def peak_mode(first, count, copy):
        step = 2 if count % 2 == 0 else 1

        def body(i, carry):
            if copy is not None:
                for k in range(step):
                    copy(i * step + k).wait()
            total = acc[...]
            for k in range(step):
                index = first + i * step + k
                total += dot(ab[index], xbuf[index])
            acc[...] = total
            return carry

        lax.fori_loop(0, count // step, body, 0)

    def pair_peak(d, k):
        index = 2 * (d - 1) * per_block + k
        acc[...] += dot(ab[index], xbuf[index]) + dot(
            ab[index + per_block], xbuf[index + per_block]
        )

    def sib_send(chip_slot, k):
        pos = 2 * chip_slot
        return pltpu.make_async_remote_copy(
            src_ref=part.at[pos * per_block + k], dst_ref=sib.at[chip_slot, k],
            send_sem=s_ssem.at[chip_slot, k], recv_sem=s_rsem.at[chip_slot, k],
            device_id=(pix, sibling), device_id_type=MESH,
        )

    def far_send(d, k):
        device = 2 * lax.rem(chip + d, n_chip) + core
        pos = 2 * (d - 1) + 1
        return pltpu.make_async_remote_copy(
            src_ref=part.at[pos * per_block + k], dst_ref=far.at[d - 1, k],
            send_sem=f_ssem.at[d - 1, k], recv_sem=f_rsem.at[d - 1, k],
            device_id=(pix, device), device_id_type=MESH,
        )

    def pair_mode(d, k):
        index = 2 * (d - 1) * per_block + k
        pix_chunks([(index, 0), (index + per_block, 1)])
        sib_send(d - 1, k).start()

    def pair_finish(d, k):
        sib_send(d - 1, k).wait_recv()
        part[(2 * (d - 1) + 1) * per_block + k] += sib[d - 1, k]
        far_send(d, k).start()

    acc[...] = jnp.zeros_like(acc)
    expand(own)
    for p in first:
        for copy in pair_x(*p):
            copy.wait()
        pair_mode(*p)
    peak_mode(own * per_block, per_block, lambda k: x_copy(own, k))
    for copy in a_out:
        copy.wait_recv()
    for copy in a_fwd:
        copy.start()
    for p in first:
        pair_finish(*p)
    for p in second:
        for copy in pair_x(*p):
            copy.wait()
    expand(near)
    for p in second:
        pair_mode(*p)
    for copy in a_fwd:
        copy.wait_recv()
    for pos in range(near):
        expand(pos)
    for p in first + second:
        pair_peak(*p)
    for p in second:
        pair_finish(*p)
    acc[:rank, :] -= dot3(split3(ga[...] * gram_b), c_ref[...])
    peak_mode(near * per_block, per_block, lambda k: x_copy(near, k))
    for p in third:
        for copy in pair_x(*p):
            copy.wait()
        pair_mode(*p)
        pair_peak(*p)
    for p in late:
        for copy in pair_x(*p):
            copy.wait()
        pair_peak(*p)

    pbuf[...] = ((acc[:rank, :] + acc[rank:, :]) * scale).reshape(pbuf.shape)
    r_out = []
    for d in range(1, n_pix):
        device = lax.rem(pix + d, n_pix)
        r_out.append(pltpu.make_async_remote_copy(
            src_ref=pbuf.at[device], dst_ref=rbuf.at[d - 1],
            send_sem=r_ssem.at[d - 1], recv_sem=r_rsem.at[d - 1],
            device_id=(device, me), device_id_type=MESH,
        ))
        r_out[-1].start()

    for p in third:
        pair_finish(*p)
    for p in late:
        pair_mode(*p)

    def single_mode(pos, send):
        step = 2 if per_block % 2 == 0 else 1

        def body(i, carry):
            first = pos * per_block + i * step
            pix_chunks([(first + k, k) for k in range(step)])
            if send:
                for k in range(step):
                    sib_send(n_chip - 1, i * step + k).start()
            return carry

        lax.fori_loop(0, per_block // step, body, 0)

    for d in range(1, n_peak):
        g_out[d - 1].wait_recv()
    gram_c = gc[0]
    for d in range(1, n_peak):
        gram_c += gc[d]
    weight = split3(gram_b * gram_c[:, :rank])
    for k in range(per_block):
        fix[k] = dot3(weight, at[own, k])
    single_mode(near, True)
    for p in late:
        pair_finish(*p)

    for d in range(1, n_pix):
        r_out[d - 1].wait_recv()
    total = pbuf[pix]
    for d in range(1, n_pix):
        total += rbuf[d - 1]
    gpeak_ref[pix] = total
    o_out = []
    for d in range(1, n_pix):
        device = lax.rem(pix + d, n_pix)
        o_out.append(pltpu.make_async_remote_copy(
            src_ref=gpeak_ref.at[pix], dst_ref=gpeak_ref.at[pix],
            send_sem=o_ssem.at[d - 1], recv_sem=o_rsem.at[d - 1],
            device_id=(device, me), device_id_type=MESH,
        ))
        o_out[-1].start()

    single_mode(own, False)

    for k in range(per_block):
        sib_send(n_chip - 1, k).wait_recv()
    for p in pairs:
        far_send(*p).wait_recv()
    for k in range(per_block):
        total = part[own * per_block + k] + sib[n_chip - 1, k]
        for d in range(1, n_chip):
            total += far[d - 1, k]
        total = total.T
        lo = k * CHUNK
        gpix_ref[:, lo:lo + half] = total[:rank] - fix[k, :, :half]
        gpix_ref[:, lo + half:lo + CHUNK] = total[rank:] - fix[k, :, half:]

    for d in range(1, n_pix):
        o_out[d - 1].wait_recv()
    for copy in a_out + a_fwd + g_out + r_out + o_out:
        copy.wait_send()
    for chip_slot in range(n_chip):
        for k in range(per_block):
            sib_send(chip_slot, k).wait_send()
    for p in pairs:
        far_send(*p).wait_send()


def place(pix_in, peak_in, pix_out, peak_out):
    pix_out[...] = pix_in[...]
    peak_out[...] = peak_in[...]


def solution(mesh):
    n_pix, n_peak = mesh.shape["pix"], mesh.shape["peak"]

    def on_device(cube, pix_factor, sec_factor, peak_factor):
        pixels, sections, peaks = cube.shape
        rank = peak_factor.shape[1]
        own = pix_factor.shape[0]
        per_block = own // CHUNK
        rows = CHUNK * sections
        n_chip = n_peak // 2
        n_far = max(n_chip - 1, 1)
        n_chunk = n_peak * per_block
        scale = 1.0 / math.sqrt(float(sections * pixels * n_pix))
        dma = pltpu.SemaphoreType.DMA
        vmem = pl.BlockSpec(memory_space=pltpu.VMEM)
        anywhere = pl.BlockSpec(memory_space=pl.ANY)
        packed = (CHUNK // 2, 2 * rank)
        grad_pix, grad_peak = pl.pallas_call(
            functools.partial(kernel, n_pix, n_peak, per_block, scale),
            out_shape=(
                jax.ShapeDtypeStruct((rank, own), F32),
                jax.ShapeDtypeStruct((n_pix, rank // n_pix, peaks), F32),
            ),
            in_specs=[anywhere, vmem, vmem, vmem],
            out_specs=(vmem, vmem),
            scratch_shapes=[
                pltpu.VMEM((n_chunk, rows, peaks), BF16),
                pltpu.VMEM((n_peak, per_block, rank, CHUNK), BF16),
                pltpu.VMEM((sections, CHUNK, CHUNK), BF16),
                pltpu.VMEM((n_chunk, 2 * rank, rows), BF16),
                pltpu.VMEM((2, rows // 2, 2 * rank), F32),
                pltpu.VMEM((n_chunk,) + packed, F32),
                pltpu.VMEM((n_chip, per_block) + packed, F32),
                pltpu.VMEM((n_far, per_block) + packed, F32),
                pltpu.VMEM((n_peak, rank, 2 * rank), F32),
                pltpu.VMEM((2 * rank, peaks), F32),
                pltpu.VMEM((n_pix, rank // n_pix, peaks), F32),
                pltpu.VMEM((n_pix - 1, rank // n_pix, peaks), F32),
                pltpu.VMEM((peaks, 2 * rank), BF16),
                pltpu.VMEM((rank, CHUNK), F32),
                pltpu.VMEM((rank, rank), F32),
                pltpu.VMEM((per_block, rank, CHUNK), F32),
                dma((n_chunk,)),
                dma((n_peak - 1,)), dma((n_peak - 1,)),
                dma((n_peak - 1,)), dma((n_peak - 1,)),
                dma((n_chip, per_block)), dma((n_chip, per_block)),
                dma((n_far, per_block)), dma((n_far, per_block)),
                dma((n_pix - 1,)), dma((n_pix - 1,)),
                dma((n_pix - 1,)), dma((n_pix - 1,)),
            ],
            compiler_params=pltpu.CompilerParams(
                collective_id=0, has_side_effects=True, vmem_limit_bytes=56 * 1024 * 1024
            ),
            name="cp_gradient",
        )(cube.reshape(pixels * sections, peaks), pix_factor.T, sec_factor, peak_factor.T)
        grad_pix, grad_peak = pl.pallas_call(
            place,
            out_shape=(
                jax.ShapeDtypeStruct((rank, own), F32),
                jax.ShapeDtypeStruct((rank, peaks), F32),
            ),
            in_specs=[vmem, vmem],
            out_specs=(vmem, vmem),
            name="place_results",
        )(grad_pix, grad_peak.reshape(rank, peaks))
        return grad_pix.T, grad_peak.T

    in_specs = (P("pix", None, "peak"), P(("pix", "peak"), None), P(), P("peak", None))
    out_specs = (P(("pix", "peak"), None), P("peak", None))
    return jax.shard_map(
        on_device, mesh=mesh, in_specs=in_specs, out_specs=out_specs, check_vma=False
    )
```

```python
import functools
import math

import jax
import jax.numpy as jnp
from jax import lax
from jax.experimental import pallas as pl
from jax.experimental.pallas import tpu as pltpu
from jax.sharding import PartitionSpec as P

MESH = pl.DeviceIdType.MESH
F32 = jnp.float32
BF16 = jnp.bfloat16
CHUNK = 256


def dot(a, b):
    return jnp.dot(a, b, preferred_element_type=F32)


def dot_nt(a, b):
    return lax.dot_general(a, b, (((1,), (1,)), ((), ())), preferred_element_type=F32)


def split3(x):
    one = x.astype(BF16)
    rest = x - one.astype(F32)
    two = rest.astype(BF16)
    return one, two, (rest - two.astype(F32)).astype(BF16)


def dot3(parts, b):
    return dot(parts[0], b) + (dot(parts[1], b) + dot(parts[2], b))


def kernel(
    n_pix, n_peak, per_block, scale,
    x_hbm, a_ref, b_ref, c_ref,
    gpix_ref, gpeak_ref,
    xbuf, at, spread, ab, part, sib, far, gc, acc, pbuf, rbuf, cc, bt, ga, fix,
    x_sem, a_ssem, a_rsem, g_ssem, g_rsem, s_ssem, s_rsem, f_ssem, f_rsem,
    r_ssem, r_rsem, o_ssem, o_rsem,
):
    rank = c_ref.shape[0]
    sections = b_ref.shape[0]
    rows = CHUNK * sections
    half = CHUNK // 2
    n_chip = n_peak // 2
    wide_r = 2 * rank
    pix = lax.axis_index("pix")
    me = lax.axis_index("peak")
    chip = me // 2
    core = lax.rem(me, 2)
    sibling = 2 * chip + 1 - core
    own = n_peak - 1
    near = n_peak - 2

    blocks = []
    for d in range(1, n_chip):
        other = lax.rem(chip + d, n_chip)
        blocks += [2 * other + 1 - core, 2 * other + core]
    blocks += [sibling, me]

    pairs = [(d, k) for k in range(per_block) for d in range(1, n_chip)]
    cuts = [len(pairs) * n // 4 for n in range(5)]
    first, second, third, late = [pairs[lo:hi] for lo, hi in zip(cuts, cuts[1:])]

    def x_copy(pos, k):
        first = (blocks[pos] * per_block + k) * rows
        return pltpu.make_async_copy(
            x_hbm.at[pl.ds(pl.multiple_of(first, rows), rows), :],
            xbuf.at[pos * per_block + k],
            x_sem.at[pos * per_block + k],
        )

    def pair_x(d, k):
        return [x_copy(2 * (d - 1), k), x_copy(2 * (d - 1) + 1, k)]

    order = [c for p in first for c in pair_x(*p)] + [x_copy(own, k) for k in range(per_block)]
    order += [c for p in second for c in pair_x(*p)] + [x_copy(near, k) for k in range(per_block)]
    order += [c for p in third + late for c in pair_x(*p)]
    for copy in order:
        copy.start()

    barrier = pltpu.get_barrier_semaphore()
    for d in range(1, n_peak):
        pl.semaphore_signal(
            barrier, inc=1, device_id=(pix, lax.rem(me + d, n_peak)), device_id_type=MESH
        )
    for d in range(1, n_pix):
        pl.semaphore_signal(
            barrier, inc=1, device_id=(lax.rem(pix + d, n_pix), me), device_id_type=MESH
        )

    for k in range(per_block):
        at[own, k] = a_ref[:, k * CHUNK:(k + 1) * CHUNK]
    ct = c_ref[...].astype(F32)
    cc[...] = jnp.concatenate([ct, ct], axis=0).T.astype(BF16)
    gc[0] = dot(c_ref[...], cc[...])

    pl.semaphore_wait(barrier, n_peak - 1 + n_pix - 1)

    def a_send(index, src, dst, device):
        return pltpu.make_async_remote_copy(
            src_ref=at.at[src], dst_ref=at.at[dst],
            send_sem=a_ssem.at[index], recv_sem=a_rsem.at[dst],
            device_id=(pix, device), device_id_type=MESH,
        )

    a_out = []
    for d in range(1, n_chip):
        device = 2 * lax.rem(chip - d + n_chip, n_chip) + core
        a_out.append(a_send(2 * (d - 1), own, 2 * (d - 1) + 1, device))
        a_out[-1].start()
    a_out.append(a_send(near, own, near, sibling))
    a_out[-1].start()
    a_fwd = [
        a_send(2 * (d - 1) + 1, 2 * (d - 1) + 1, 2 * (d - 1), sibling) for d in range(1, n_chip)
    ]

    g_out = []
    for d in range(1, n_peak):
        g_out.append(pltpu.make_async_remote_copy(
            src_ref=gc.at[0], dst_ref=gc.at[d],
            send_sem=g_ssem.at[d - 1], recv_sem=g_rsem.at[d - 1],
            device_id=(pix, lax.rem(me + d, n_peak)), device_id_type=MESH,
        ))
        g_out[-1].start()

    row = lax.broadcasted_iota(jnp.int32, (rank, rank), 0)
    col = lax.broadcasted_iota(jnp.int32, (rank, rank), 1)
    eye = (row == col).astype(F32).astype(BF16)
    row = lax.broadcasted_iota(jnp.int32, (rank, wide_r), 0)
    col = lax.broadcasted_iota(jnp.int32, (rank, wide_r), 1)
    eye2 = ((row == col) | (row + rank == col)).astype(F32).astype(BF16)
    b_f = b_ref[...].astype(F32)
    b_tiled = jnp.broadcast_to(b_f[None], (CHUNK // sections, sections, rank))
    b_tiled = b_tiled.reshape(CHUNK, rank)
    bt[...] = dot_nt(eye, b_tiled.astype(BF16))
    bb = dot(b_ref[...], eye2)
    lead = lax.broadcasted_iota(jnp.int32, (CHUNK, rank), 0) < sections
    b_once = jnp.where(lead, b_tiled, 0.0).astype(BF16)
    gram_b = dot(dot_nt(eye, b_once).astype(BF16), b_once)
    row = lax.broadcasted_iota(jnp.int32, (CHUNK, CHUNK), 0)
    col = lax.broadcasted_iota(jnp.int32, (CHUNK, CHUNK), 1) // sections
    for j in range(sections):
        spread[j] = (row == col + j * (CHUNK // sections)).astype(F32).astype(BF16)
    ga[...] = jnp.zeros_like(ga)

    lane_lo = lax.broadcasted_iota(jnp.int32, (half * sections, wide_r), 1) < rank
    bb_all = jnp.broadcast_to(bb[None], (half, sections, wide_r))
    sub = lax.broadcasted_iota(jnp.int32, (half // sections, sections, wide_r), 1)

    def roll(x, shift):
        return pltpu.roll(x, shift % sections, 1)

    def section_sum(x):
        level = [x[:, n] for n in range(sections)]
        step = sections // 2
        while step >= 1:
            mask = lax.rem(sub, 2 * step) < step
            pairs_of = list(zip(level[:step], level[step:]))
            if 2 * step == sections:
                level = [
                    jnp.where(mask, one, two) + roll(jnp.where(mask, two, one), step)
                    for one, two in pairs_of
                ]
            else:
                level = [
                    jnp.where(mask, one + roll(one, -step), two + roll(two, step))
                    for one, two in pairs_of
                ]
            step //= 2
        return level[0]

    def pix_chunks(todo):
        for index in todo:
            full = dot(xbuf[index], cc[...])
            both = jnp.where(lane_lo, full[: half * sections], full[half * sections:])
            both = both.reshape(half, sections, wide_r) * bb_all
            both = both.reshape(half // sections, sections, sections, wide_r)
            part[index] = section_sum(both).reshape(half, wide_r)

    def expand(pos):
        stacked = at[pos].reshape(per_block * rank, CHUNK)
        for j in range(sections):
            product = dot(stacked, spread[j]).reshape(per_block, rank, CHUNK) * bt[...][None]
            high = product.astype(BF16)
            low = (product - high.astype(F32)).astype(BF16)
            first = pos * per_block
            ab[first:first + per_block, :rank, j * CHUNK:(j + 1) * CHUNK] = high
            ab[first:first + per_block, rank:, j * CHUNK:(j + 1) * CHUNK] = low
        for k in range(per_block):
            ga[...] += dot_nt(at[pos, k], at[pos, k])

    def peak_mode(first, count, copy):
        step = 2 if count % 2 == 0 else 1

        def body(i, carry):
            if copy is not None:
                for k in range(step):
                    copy(i * step + k).wait()
            total = acc[...]
            for k in range(step):
                index = first + i * step + k
                total += dot(ab[index], xbuf[index])
            acc[...] = total
            return carry

        lax.fori_loop(0, count // step, body, 0)

    def pair_peak(d, k):
        index = 2 * (d - 1) * per_block + k
        acc[...] += dot(ab[index], xbuf[index]) + dot(
            ab[index + per_block], xbuf[index + per_block]
        )

    def sib_send(chip_slot, k):
        pos = 2 * chip_slot
        return pltpu.make_async_remote_copy(
            src_ref=part.at[pos * per_block + k], dst_ref=sib.at[chip_slot, k],
            send_sem=s_ssem.at[chip_slot, k], recv_sem=s_rsem.at[chip_slot, k],
            device_id=(pix, sibling), device_id_type=MESH,
        )

    def far_send(d, k):
        device = 2 * lax.rem(chip + d, n_chip) + core
        pos = 2 * (d - 1) + 1
        return pltpu.make_async_remote_copy(
            src_ref=part.at[pos * per_block + k], dst_ref=far.at[d - 1, k],
            send_sem=f_ssem.at[d - 1, k], recv_sem=f_rsem.at[d - 1, k],
            device_id=(pix, device), device_id_type=MESH,
        )

    def pair_mode(d, k):
        index = 2 * (d - 1) * per_block + k
        pix_chunks([index, index + per_block])
        sib_send(d - 1, k).start()

    def pair_finish(d, k):
        sib_send(d - 1, k).wait_recv()
        part[(2 * (d - 1) + 1) * per_block + k] += sib[d - 1, k]
        far_send(d, k).start()

    acc[...] = jnp.zeros_like(acc)
    expand(own)
    for p in first:
        for copy in pair_x(*p):
            copy.wait()
        pair_mode(*p)
    peak_mode(own * per_block, per_block, lambda k: x_copy(own, k))
    for copy in a_out:
        copy.wait_recv()
    for copy in a_fwd:
        copy.start()
    for p in first:
        pair_finish(*p)
    for p in second:
        for copy in pair_x(*p):
            copy.wait()
    expand(near)
    for p in second:
        pair_mode(*p)
    for copy in a_fwd:
        copy.wait_recv()
    for pos in range(near):
        expand(pos)
    for p in first + second:
        pair_peak(*p)
    for p in second:
        pair_finish(*p)
    acc[:rank, :] -= dot3(split3(ga[...] * gram_b), c_ref[...])
    peak_mode(near * per_block, per_block, lambda k: x_copy(near, k))
    for p in third:
        for copy in pair_x(*p):
            copy.wait()
        pair_mode(*p)
        pair_peak(*p)
    for p in late:
        for copy in pair_x(*p):
            copy.wait()
        pair_peak(*p)

    pbuf[...] = ((acc[:rank, :] + acc[rank:, :]) * scale).reshape(pbuf.shape)
    r_out = []
    for d in range(1, n_pix):
        device = lax.rem(pix + d, n_pix)
        r_out.append(pltpu.make_async_remote_copy(
            src_ref=pbuf.at[device], dst_ref=rbuf.at[d - 1],
            send_sem=r_ssem.at[d - 1], recv_sem=r_rsem.at[d - 1],
            device_id=(device, me), device_id_type=MESH,
        ))
        r_out[-1].start()

    for p in third:
        pair_finish(*p)
    for p in late:
        pair_mode(*p)

    def single_mode(pos, send):
        step = 2 if per_block % 2 == 0 else 1

        def body(i, carry):
            first = pos * per_block + i * step
            pix_chunks([first + k for k in range(step)])
            if send:
                for k in range(step):
                    sib_send(n_chip - 1, i * step + k).start()
            return carry

        lax.fori_loop(0, per_block // step, body, 0)

    for d in range(1, n_peak):
        g_out[d - 1].wait_recv()
    gram_c = gc[0]
    for d in range(1, n_peak):
        gram_c += gc[d]
    weight = split3(gram_b * gram_c[:, :rank])
    for k in range(per_block):
        fix[k] = dot3(weight, at[own, k])
    single_mode(near, True)
    for p in late:
        pair_finish(*p)

    for d in range(1, n_pix):
        r_out[d - 1].wait_recv()
    total = pbuf[pix]
    for d in range(1, n_pix):
        total += rbuf[d - 1]
    gpeak_ref[pix] = total
    o_out = []
    for d in range(1, n_pix):
        device = lax.rem(pix + d, n_pix)
        o_out.append(pltpu.make_async_remote_copy(
            src_ref=gpeak_ref.at[pix], dst_ref=gpeak_ref.at[pix],
            send_sem=o_ssem.at[d - 1], recv_sem=o_rsem.at[d - 1],
            device_id=(device, me), device_id_type=MESH,
        ))
        o_out[-1].start()

    single_mode(own, False)

    for k in range(per_block):
        sib_send(n_chip - 1, k).wait_recv()
    for p in pairs:
        far_send(*p).wait_recv()
    for k in range(per_block):
        total = part[own * per_block + k] + sib[n_chip - 1, k]
        for d in range(1, n_chip):
            total += far[d - 1, k]
        total = total.T
        lo = k * CHUNK
        gpix_ref[:, lo:lo + half] = total[:rank] - fix[k, :, :half]
        gpix_ref[:, lo + half:lo + CHUNK] = total[rank:] - fix[k, :, half:]

    for d in range(1, n_pix):
        o_out[d - 1].wait_recv()
    for copy in a_out + a_fwd + g_out + r_out + o_out:
        copy.wait_send()
    for chip_slot in range(n_chip):
        for k in range(per_block):
            sib_send(chip_slot, k).wait_send()
    for p in pairs:
        far_send(*p).wait_send()


def place(pix_in, peak_in, pix_out, peak_out):
    pix_out[...] = pix_in[...]
    peak_out[...] = peak_in[...]


def solution(mesh):
    n_pix, n_peak = mesh.shape["pix"], mesh.shape["peak"]

    def on_device(cube, pix_factor, sec_factor, peak_factor):
        pixels, sections, peaks = cube.shape
        rank = peak_factor.shape[1]
        own = pix_factor.shape[0]
        per_block = own // CHUNK
        rows = CHUNK * sections
        n_chip = n_peak // 2
        n_far = max(n_chip - 1, 1)
        n_chunk = n_peak * per_block
        scale = 1.0 / math.sqrt(float(sections * pixels * n_pix))
        dma = pltpu.SemaphoreType.DMA
        vmem = pl.BlockSpec(memory_space=pltpu.VMEM)
        anywhere = pl.BlockSpec(memory_space=pl.ANY)
        packed = (CHUNK // 2, 2 * rank)
        grad_pix, grad_peak = pl.pallas_call(
            functools.partial(kernel, n_pix, n_peak, per_block, scale),
            out_shape=(
                jax.ShapeDtypeStruct((rank, own), F32),
                jax.ShapeDtypeStruct((n_pix, rank // n_pix, peaks), F32),
            ),
            in_specs=[anywhere, vmem, vmem, vmem],
            out_specs=(vmem, vmem),
            scratch_shapes=[
                pltpu.VMEM((n_chunk, rows, peaks), BF16),
                pltpu.VMEM((n_peak, per_block, rank, CHUNK), BF16),
                pltpu.VMEM((sections, CHUNK, CHUNK), BF16),
                pltpu.VMEM((n_chunk, 2 * rank, rows), BF16),
                pltpu.VMEM((n_chunk,) + packed, F32),
                pltpu.VMEM((n_chip, per_block) + packed, F32),
                pltpu.VMEM((n_far, per_block) + packed, F32),
                pltpu.VMEM((n_peak, rank, 2 * rank), F32),
                pltpu.VMEM((2 * rank, peaks), F32),
                pltpu.VMEM((n_pix, rank // n_pix, peaks), F32),
                pltpu.VMEM((n_pix - 1, rank // n_pix, peaks), F32),
                pltpu.VMEM((peaks, 2 * rank), BF16),
                pltpu.VMEM((rank, CHUNK), F32),
                pltpu.VMEM((rank, rank), F32),
                pltpu.VMEM((per_block, rank, CHUNK), F32),
                dma((n_chunk,)),
                dma((n_peak - 1,)), dma((n_peak - 1,)),
                dma((n_peak - 1,)), dma((n_peak - 1,)),
                dma((n_chip, per_block)), dma((n_chip, per_block)),
                dma((n_far, per_block)), dma((n_far, per_block)),
                dma((n_pix - 1,)), dma((n_pix - 1,)),
                dma((n_pix - 1,)), dma((n_pix - 1,)),
            ],
            compiler_params=pltpu.CompilerParams(
                collective_id=0, has_side_effects=True, vmem_limit_bytes=56 * 1024 * 1024
            ),
            name="cp_gradient",
        )(cube.reshape(pixels * sections, peaks), pix_factor.T, sec_factor, peak_factor.T)
        grad_pix, grad_peak = pl.pallas_call(
            place,
            out_shape=(
                jax.ShapeDtypeStruct((rank, own), F32),
                jax.ShapeDtypeStruct((rank, peaks), F32),
            ),
            in_specs=[vmem, vmem],
            out_specs=(vmem, vmem),
            name="place_results",
        )(grad_pix, grad_peak.reshape(rank, peaks))
        return grad_pix.T, grad_peak.T

    in_specs = (P("pix", None, "peak"), P(("pix", "peak"), None), P(), P("peak", None))
    out_specs = (P(("pix", "peak"), None), P("peak", None))
    return jax.shard_map(
        on_device, mesh=mesh, in_specs=in_specs, out_specs=out_specs, check_vma=False
    )
```

```python
import functools
import math

import jax
import jax.numpy as jnp
from jax import lax
from jax.experimental import pallas as pl
from jax.experimental.pallas import tpu as pltpu
from jax.sharding import PartitionSpec as P

MESH = pl.DeviceIdType.MESH
F32 = jnp.float32
BF16 = jnp.bfloat16
CHUNK = 256


def dot(a, b):
    return jnp.dot(a, b, preferred_element_type=F32)


def dot_nt(a, b):
    return lax.dot_general(a, b, (((1,), (1,)), ((), ())), preferred_element_type=F32)


def split3(x):
    one = x.astype(BF16)
    rest = x - one.astype(F32)
    two = rest.astype(BF16)
    return one, two, (rest - two.astype(F32)).astype(BF16)


def dot3(parts, b):
    return dot(parts[0], b) + (dot(parts[1], b) + dot(parts[2], b))


def kernel(
    n_pix, n_peak, per_block, scale,
    x_hbm, a_ref, b_ref, c_ref,
    gpix_ref, gpeak_ref,
    xbuf, at, spread, ab, part, sib, far, gc, acc, pbuf, rbuf, cc, bt, ga, fix,
    x_sem, a_ssem, a_rsem, g_ssem, g_rsem, s_ssem, s_rsem, f_ssem, f_rsem,
    r_ssem, r_rsem, o_ssem, o_rsem,
):
    rank = c_ref.shape[0]
    sections = b_ref.shape[0]
    rows = CHUNK * sections
    half = CHUNK // 2
    n_chip = n_peak // 2
    wide_r = 2 * rank
    pix = lax.axis_index("pix")
    me = lax.axis_index("peak")
    chip = me // 2
    core = lax.rem(me, 2)
    sibling = 2 * chip + 1 - core
    own = n_peak - 1
    near = n_peak - 2

    blocks = []
    for d in range(1, n_chip):
        other = lax.rem(chip + d, n_chip)
        blocks += [2 * other + 1 - core, 2 * other + core]
    blocks += [sibling, me]

    pairs = [(d, k) for k in range(per_block) for d in range(1, n_chip)]
    cuts = [len(pairs) * n // 4 for n in range(5)]
    first, second, third, late = [pairs[lo:hi] for lo, hi in zip(cuts, cuts[1:])]

    def x_copy(pos, k):
        first = (blocks[pos] * per_block + k) * rows
        return pltpu.make_async_copy(
            x_hbm.at[pl.ds(pl.multiple_of(first, rows), rows), :],
            xbuf.at[pos * per_block + k],
            x_sem.at[pos * per_block + k],
        )

    def pair_x(d, k):
        return [x_copy(2 * (d - 1), k), x_copy(2 * (d - 1) + 1, k)]

    order = [c for p in first for c in pair_x(*p)] + [x_copy(own, k) for k in range(per_block)]
    order += [c for p in second for c in pair_x(*p)] + [x_copy(near, k) for k in range(per_block)]
    order += [c for p in third + late for c in pair_x(*p)]
    for copy in order:
        copy.start()

    barrier = pltpu.get_barrier_semaphore()
    for d in range(1, n_peak):
        pl.semaphore_signal(
            barrier, inc=1, device_id=(pix, lax.rem(me + d, n_peak)), device_id_type=MESH
        )
    for d in range(1, n_pix):
        pl.semaphore_signal(
            barrier, inc=1, device_id=(lax.rem(pix + d, n_pix), me), device_id_type=MESH
        )

    for k in range(per_block):
        at[own, k] = a_ref[:, k * CHUNK:(k + 1) * CHUNK]
    ct = c_ref[...].astype(F32)
    cc[...] = jnp.concatenate([ct, ct], axis=0).T.astype(BF16)
    gc[0] = dot(c_ref[...], cc[...])

    row = lax.broadcasted_iota(jnp.int32, (rank, rank), 0)
    col = lax.broadcasted_iota(jnp.int32, (rank, rank), 1)
    eye = (row == col).astype(F32).astype(BF16)
    row = lax.broadcasted_iota(jnp.int32, (rank, wide_r), 0)
    col = lax.broadcasted_iota(jnp.int32, (rank, wide_r), 1)
    eye2 = ((row == col) | (row + rank == col)).astype(F32).astype(BF16)
    b_f = b_ref[...].astype(F32)
    b_tiled = jnp.broadcast_to(b_f[None], (CHUNK // sections, sections, rank))
    b_tiled = b_tiled.reshape(CHUNK, rank)
    bt[...] = dot_nt(eye, b_tiled.astype(BF16))
    bb = dot(b_ref[...], eye2)
    lead = lax.broadcasted_iota(jnp.int32, (CHUNK, rank), 0) < sections
    b_once = jnp.where(lead, b_tiled, 0.0).astype(BF16)
    gram_b = dot(dot_nt(eye, b_once).astype(BF16), b_once)
    row = lax.broadcasted_iota(jnp.int32, (CHUNK, CHUNK), 0)
    col = lax.broadcasted_iota(jnp.int32, (CHUNK, CHUNK), 1) // sections
    for j in range(sections):
        spread[j] = (row == col + j * (CHUNK // sections)).astype(F32).astype(BF16)
    ga[...] = jnp.zeros_like(ga)

    lane_lo = lax.broadcasted_iota(jnp.int32, (half * sections, wide_r), 1) < rank
    bb_all = jnp.broadcast_to(bb[None], (half, sections, wide_r))
    sub = lax.broadcasted_iota(jnp.int32, (half // sections, sections, wide_r), 1)

    def roll(x, shift):
        return pltpu.roll(x, shift % sections, 1)

    def section_sum(x):
        level = [x[:, n] for n in range(sections)]
        step = sections // 2
        while step >= 1:
            mask = lax.rem(sub, 2 * step) < step
            pairs_of = list(zip(level[:step], level[step:]))
            if 2 * step == sections:
                level = [
                    jnp.where(mask, one, two) + roll(jnp.where(mask, two, one), step)
                    for one, two in pairs_of
                ]
            else:
                level = [
                    jnp.where(mask, one + roll(one, -step), two + roll(two, step))
                    for one, two in pairs_of
                ]
            step //= 2
        return level[0]

    def pix_chunks(todo):
        for index in todo:
            full = dot(xbuf[index], cc[...])
            both = jnp.where(lane_lo, full[: half * sections], full[half * sections:])
            both = both.reshape(half, sections, wide_r) * bb_all
            both = both.reshape(half // sections, sections, sections, wide_r)
            part[index] = section_sum(both).reshape(half, wide_r)

    def expand(pos):
        stacked = at[pos].reshape(per_block * rank, CHUNK)
        for j in range(sections):
            product = dot(stacked, spread[j]).reshape(per_block, rank, CHUNK) * bt[...][None]
            high = product.astype(BF16)
            low = (product - high.astype(F32)).astype(BF16)
            first = pos * per_block
            ab[first:first + per_block, :rank, j * CHUNK:(j + 1) * CHUNK] = high
            ab[first:first + per_block, rank:, j * CHUNK:(j + 1) * CHUNK] = low
        for k in range(per_block):
            ga[...] += dot_nt(at[pos, k], at[pos, k])

    def peak_mode(first, count, copy):
        step = 2 if count % 2 == 0 else 1

        def body(i, carry):
            if copy is not None:
                for k in range(step):
                    copy(i * step + k).wait()
            total = acc[...]
            for k in range(step):
                index = first + i * step + k
                total += dot(ab[index], xbuf[index])
            acc[...] = total
            return carry

        lax.fori_loop(0, count // step, body, 0)

    def pair_peak(d, k):
        index = 2 * (d - 1) * per_block + k
        acc[...] += dot(ab[index], xbuf[index]) + dot(
            ab[index + per_block], xbuf[index + per_block]
        )

    def sib_send(chip_slot, k):
        pos = 2 * chip_slot
        return pltpu.make_async_remote_copy(
            src_ref=part.at[pos * per_block + k], dst_ref=sib.at[chip_slot, k],
            send_sem=s_ssem.at[chip_slot, k], recv_sem=s_rsem.at[chip_slot, k],
            device_id=(pix, sibling), device_id_type=MESH,
        )

    def far_send(d, k):
        device = 2 * lax.rem(chip + d, n_chip) + core
        pos = 2 * (d - 1) + 1
        return pltpu.make_async_remote_copy(
            src_ref=part.at[pos * per_block + k], dst_ref=far.at[d - 1, k],
            send_sem=f_ssem.at[d - 1, k], recv_sem=f_rsem.at[d - 1, k],
            device_id=(pix, device), device_id_type=MESH,
        )

    def pair_mode(d, k):
        index = 2 * (d - 1) * per_block + k
        pix_chunks([index, index + per_block])
        sib_send(d - 1, k).start()

    def pair_finish(d, k):
        sib_send(d - 1, k).wait_recv()
        part[(2 * (d - 1) + 1) * per_block + k] += sib[d - 1, k]
        far_send(d, k).start()

    acc[...] = jnp.zeros_like(acc)
    expand(own)

    pl.semaphore_wait(barrier, n_peak - 1 + n_pix - 1)

    def a_send(index, src, dst, device):
        return pltpu.make_async_remote_copy(
            src_ref=at.at[src], dst_ref=at.at[dst],
            send_sem=a_ssem.at[index], recv_sem=a_rsem.at[dst],
            device_id=(pix, device), device_id_type=MESH,
        )

    a_out = []
    for d in range(1, n_chip):
        device = 2 * lax.rem(chip - d + n_chip, n_chip) + core
        a_out.append(a_send(2 * (d - 1), own, 2 * (d - 1) + 1, device))
        a_out[-1].start()
    a_out.append(a_send(near, own, near, sibling))
    a_out[-1].start()
    a_fwd = [
        a_send(2 * (d - 1) + 1, 2 * (d - 1) + 1, 2 * (d - 1), sibling) for d in range(1, n_chip)
    ]

    g_out = []
    for d in range(1, n_peak):
        g_out.append(pltpu.make_async_remote_copy(
            src_ref=gc.at[0], dst_ref=gc.at[d],
            send_sem=g_ssem.at[d - 1], recv_sem=g_rsem.at[d - 1],
            device_id=(pix, lax.rem(me + d, n_peak)), device_id_type=MESH,
        ))
        g_out[-1].start()

    for p in first:
        for copy in pair_x(*p):
            copy.wait()
        pair_mode(*p)
    peak_mode(own * per_block, per_block, lambda k: x_copy(own, k))
    for copy in a_out:
        copy.wait_recv()
    for copy in a_fwd:
        copy.start()
    for p in first:
        pair_finish(*p)
    for p in second:
        for copy in pair_x(*p):
            copy.wait()
    expand(near)
    for p in second:
        pair_mode(*p)
    for copy in a_fwd:
        copy.wait_recv()
    for pos in range(near):
        expand(pos)
    for p in first + second:
        pair_peak(*p)
    for p in second:
        pair_finish(*p)
    acc[:rank, :] -= dot3(split3(ga[...] * gram_b), c_ref[...])
    peak_mode(near * per_block, per_block, lambda k: x_copy(near, k))
    for p in third + late:
        for copy in pair_x(*p):
            copy.wait()
        pair_peak(*p)

    pbuf[...] = ((acc[:rank, :] + acc[rank:, :]) * scale).reshape(pbuf.shape)
    r_out = []
    for d in range(1, n_pix):
        device = lax.rem(pix + d, n_pix)
        r_out.append(pltpu.make_async_remote_copy(
            src_ref=pbuf.at[device], dst_ref=rbuf.at[d - 1],
            send_sem=r_ssem.at[d - 1], recv_sem=r_rsem.at[d - 1],
            device_id=(device, me), device_id_type=MESH,
        ))
        r_out[-1].start()

    for n, p in enumerate(third + late):
        pair_mode(*p)
        if n > 0:
            pair_finish(*(third + late)[n - 1])

    def single_mode(pos, send):
        step = 2 if per_block % 2 == 0 else 1

        def body(i, carry):
            first = pos * per_block + i * step
            pix_chunks([first + k for k in range(step)])
            if send:
                for k in range(step):
                    sib_send(n_chip - 1, i * step + k).start()
            return carry

        lax.fori_loop(0, per_block // step, body, 0)

    for d in range(1, n_peak):
        g_out[d - 1].wait_recv()
    gram_c = gc[0]
    for d in range(1, n_peak):
        gram_c += gc[d]
    weight = split3(gram_b * gram_c[:, :rank])
    for k in range(per_block):
        fix[k] = dot3(weight, at[own, k])
    for p in late[-1:]:
        pair_finish(*p)
    single_mode(near, True)

    for d in range(1, n_pix):
        r_out[d - 1].wait_recv()
    total = pbuf[pix]
    for d in range(1, n_pix):
        total += rbuf[d - 1]
    gpeak_ref[pix] = total
    o_out = []
    for d in range(1, n_pix):
        device = lax.rem(pix + d, n_pix)
        o_out.append(pltpu.make_async_remote_copy(
            src_ref=gpeak_ref.at[pix], dst_ref=gpeak_ref.at[pix],
            send_sem=o_ssem.at[d - 1], recv_sem=o_rsem.at[d - 1],
            device_id=(device, me), device_id_type=MESH,
        ))
        o_out[-1].start()

    single_mode(own, False)

    for k in range(per_block):
        sib_send(n_chip - 1, k).wait_recv()
    for p in pairs:
        far_send(*p).wait_recv()
    for k in range(per_block):
        total = part[own * per_block + k] + sib[n_chip - 1, k]
        for d in range(1, n_chip):
            total += far[d - 1, k]
        total = total.T
        lo = k * CHUNK
        gpix_ref[:, lo:lo + half] = total[:rank] - fix[k, :, :half]
        gpix_ref[:, lo + half:lo + CHUNK] = total[rank:] - fix[k, :, half:]

    for d in range(1, n_pix):
        o_out[d - 1].wait_recv()
    for copy in a_out + a_fwd + g_out + r_out + o_out:
        copy.wait_send()
    for chip_slot in range(n_chip):
        for k in range(per_block):
            sib_send(chip_slot, k).wait_send()
    for p in pairs:
        far_send(*p).wait_send()


def place(pix_in, peak_in, pix_out, peak_out):
    pix_out[...] = pix_in[...]
    peak_out[...] = peak_in[...]


def solution(mesh):
    n_pix, n_peak = mesh.shape["pix"], mesh.shape["peak"]

    def on_device(cube, pix_factor, sec_factor, peak_factor):
        pixels, sections, peaks = cube.shape
        rank = peak_factor.shape[1]
        own = pix_factor.shape[0]
        per_block = own // CHUNK
        rows = CHUNK * sections
        n_chip = n_peak // 2
        n_far = max(n_chip - 1, 1)
        n_chunk = n_peak * per_block
        scale = 1.0 / math.sqrt(float(sections * pixels * n_pix))
        dma = pltpu.SemaphoreType.DMA
        vmem = pl.BlockSpec(memory_space=pltpu.VMEM)
        anywhere = pl.BlockSpec(memory_space=pl.ANY)
        packed = (CHUNK // 2, 2 * rank)
        grad_pix, grad_peak = pl.pallas_call(
            functools.partial(kernel, n_pix, n_peak, per_block, scale),
            out_shape=(
                jax.ShapeDtypeStruct((rank, own), F32),
                jax.ShapeDtypeStruct((n_pix, rank // n_pix, peaks), F32),
            ),
            in_specs=[anywhere, vmem, vmem, vmem],
            out_specs=(vmem, vmem),
            scratch_shapes=[
                pltpu.VMEM((n_chunk, rows, peaks), BF16),
                pltpu.VMEM((n_peak, per_block, rank, CHUNK), BF16),
                pltpu.VMEM((sections, CHUNK, CHUNK), BF16),
                pltpu.VMEM((n_chunk, 2 * rank, rows), BF16),
                pltpu.VMEM((n_chunk,) + packed, F32),
                pltpu.VMEM((n_chip, per_block) + packed, F32),
                pltpu.VMEM((n_far, per_block) + packed, F32),
                pltpu.VMEM((n_peak, rank, 2 * rank), F32),
                pltpu.VMEM((2 * rank, peaks), F32),
                pltpu.VMEM((n_pix, rank // n_pix, peaks), F32),
                pltpu.VMEM((n_pix - 1, rank // n_pix, peaks), F32),
                pltpu.VMEM((peaks, 2 * rank), BF16),
                pltpu.VMEM((rank, CHUNK), F32),
                pltpu.VMEM((rank, rank), F32),
                pltpu.VMEM((per_block, rank, CHUNK), F32),
                dma((n_chunk,)),
                dma((n_peak - 1,)), dma((n_peak - 1,)),
                dma((n_peak - 1,)), dma((n_peak - 1,)),
                dma((n_chip, per_block)), dma((n_chip, per_block)),
                dma((n_far, per_block)), dma((n_far, per_block)),
                dma((n_pix - 1,)), dma((n_pix - 1,)),
                dma((n_pix - 1,)), dma((n_pix - 1,)),
            ],
            compiler_params=pltpu.CompilerParams(
                collective_id=0, has_side_effects=True, vmem_limit_bytes=56 * 1024 * 1024
            ),
            name="cp_gradient",
        )(cube.reshape(pixels * sections, peaks), pix_factor.T, sec_factor, peak_factor.T)
        grad_pix, grad_peak = pl.pallas_call(
            place,
            out_shape=(
                jax.ShapeDtypeStruct((rank, own), F32),
                jax.ShapeDtypeStruct((rank, peaks), F32),
            ),
            in_specs=[vmem, vmem],
            out_specs=(vmem, vmem),
            name="place_results",
        )(grad_pix, grad_peak.reshape(rank, peaks))
        return grad_pix.T, grad_peak.T

    in_specs = (P("pix", None, "peak"), P(("pix", "peak"), None), P(), P("peak", None))
    out_specs = (P(("pix", "peak"), None), P("peak", None))
    return jax.shard_map(
        on_device, mesh=mesh, in_specs=in_specs, out_specs=out_specs, check_vma=False
    )
```

```python
import functools
import math

import jax
import jax.numpy as jnp
from jax import lax
from jax.experimental import pallas as pl
from jax.experimental.pallas import tpu as pltpu
from jax.sharding import PartitionSpec as P

MESH = pl.DeviceIdType.MESH
F32 = jnp.float32
BF16 = jnp.bfloat16
CHUNK = 256


def dot(a, b):
    return jnp.dot(a, b, preferred_element_type=F32)


def dot_nt(a, b):
    return lax.dot_general(a, b, (((1,), (1,)), ((), ())), preferred_element_type=F32)


def split3(x):
    one = x.astype(BF16)
    rest = x - one.astype(F32)
    two = rest.astype(BF16)
    return one, two, (rest - two.astype(F32)).astype(BF16)


def dot3(parts, b):
    return dot(parts[0], b) + (dot(parts[1], b) + dot(parts[2], b))


def kernel(
    n_pix, n_peak, per_block, scale,
    x_hbm, a_ref, b_ref, c_ref,
    gpix_ref, gpeak_ref,
    xbuf, at, spread, ab, part, sib, far, gc, acc, pbuf, rbuf, cc, bt, ga, fix,
    x_sem, a_ssem, a_rsem, g_ssem, g_rsem, s_ssem, s_rsem, f_ssem, f_rsem,
    r_ssem, r_rsem, o_ssem, o_rsem,
):
    rank = c_ref.shape[0]
    sections = b_ref.shape[0]
    rows = CHUNK * sections
    half = CHUNK // 2
    n_chip = n_peak // 2
    wide_r = 2 * rank
    pix = lax.axis_index("pix")
    me = lax.axis_index("peak")
    chip = me // 2
    core = lax.rem(me, 2)
    sibling = 2 * chip + 1 - core
    own = n_peak - 1
    near = n_peak - 2

    blocks = []
    for d in range(1, n_chip):
        other = lax.rem(chip + d, n_chip)
        blocks += [2 * other + 1 - core, 2 * other + core]
    blocks += [sibling, me]

    pairs = [(d, k) for k in range(per_block) for d in range(1, n_chip)]
    cuts = [len(pairs) * n // 4 for n in range(5)]
    first, second, third, late = [pairs[lo:hi] for lo, hi in zip(cuts, cuts[1:])]

    def x_copy(pos, k):
        first = (blocks[pos] * per_block + k) * rows
        return pltpu.make_async_copy(
            x_hbm.at[pl.ds(pl.multiple_of(first, rows), rows), :],
            xbuf.at[pos * per_block + k],
            x_sem.at[pos * per_block + k],
        )

    def pair_x(d, k):
        return [x_copy(2 * (d - 1), k), x_copy(2 * (d - 1) + 1, k)]

    order = [c for p in first for c in pair_x(*p)] + [x_copy(own, k) for k in range(per_block)]
    order += [c for p in second for c in pair_x(*p)] + [x_copy(near, k) for k in range(per_block)]
    order += [c for p in third + late for c in pair_x(*p)]
    for copy in order:
        copy.start()

    barrier = pltpu.get_barrier_semaphore()
    for d in range(1, n_peak):
        pl.semaphore_signal(
            barrier, inc=1, device_id=(pix, lax.rem(me + d, n_peak)), device_id_type=MESH
        )
    for d in range(1, n_pix):
        pl.semaphore_signal(
            barrier, inc=1, device_id=(lax.rem(pix + d, n_pix), me), device_id_type=MESH
        )

    for k in range(per_block):
        at[own, k] = a_ref[:, k * CHUNK:(k + 1) * CHUNK]
    ct = c_ref[...].astype(F32)
    cc[...] = jnp.concatenate([ct, ct], axis=0).T.astype(BF16)
    gc[0] = dot(c_ref[...], cc[...])

    row = lax.broadcasted_iota(jnp.int32, (rank, rank), 0)
    col = lax.broadcasted_iota(jnp.int32, (rank, rank), 1)
    eye = (row == col).astype(F32).astype(BF16)
    row = lax.broadcasted_iota(jnp.int32, (rank, wide_r), 0)
    col = lax.broadcasted_iota(jnp.int32, (rank, wide_r), 1)
    eye2 = ((row == col) | (row + rank == col)).astype(F32).astype(BF16)
    b_f = b_ref[...].astype(F32)
    b_tiled = jnp.broadcast_to(b_f[None], (CHUNK // sections, sections, rank))
    b_tiled = b_tiled.reshape(CHUNK, rank)
    bt[...] = dot_nt(eye, b_tiled.astype(BF16))
    bb = dot(b_ref[...], eye2)
    lead = lax.broadcasted_iota(jnp.int32, (CHUNK, rank), 0) < sections
    b_once = jnp.where(lead, b_tiled, 0.0).astype(BF16)
    gram_b = dot(dot_nt(eye, b_once).astype(BF16), b_once)
    row = lax.broadcasted_iota(jnp.int32, (CHUNK, CHUNK), 0)
    col = lax.broadcasted_iota(jnp.int32, (CHUNK, CHUNK), 1) // sections
    for j in range(sections):
        spread[j] = (row == col + j * (CHUNK // sections)).astype(F32).astype(BF16)
    ga[...] = jnp.zeros_like(ga)

    lane_lo = lax.broadcasted_iota(jnp.int32, (half * sections, wide_r), 1) < rank
    bb_all = jnp.broadcast_to(bb[None], (half, sections, wide_r))
    sub = lax.broadcasted_iota(jnp.int32, (half // sections, sections, wide_r), 1)

    def roll(x, shift):
        return pltpu.roll(x, shift % sections, 1)

    def section_sum(x):
        level = [x[:, n] for n in range(sections)]
        step = sections // 2
        while step >= 1:
            mask = lax.rem(sub, 2 * step) < step
            pairs_of = list(zip(level[:step], level[step:]))
            if 2 * step == sections:
                level = [
                    jnp.where(mask, one, two) + roll(jnp.where(mask, two, one), step)
                    for one, two in pairs_of
                ]
            else:
                level = [
                    jnp.where(mask, one + roll(one, -step), two + roll(two, step))
                    for one, two in pairs_of
                ]
            step //= 2
        return level[0]

    def pix_chunks(todo):
        for index in todo:
            full = dot(xbuf[index], cc[...])
            both = jnp.where(lane_lo, full[: half * sections], full[half * sections:])
            both = both.reshape(half, sections, wide_r) * bb_all
            both = both.reshape(half // sections, sections, sections, wide_r)
            part[index] = section_sum(both).reshape(half, wide_r)

    def expand(pos):
        stacked = at[pos].reshape(per_block * rank, CHUNK)
        for j in range(sections):
            product = dot(stacked, spread[j]).reshape(per_block, rank, CHUNK) * bt[...][None]
            high = product.astype(BF16)
            low = (product - high.astype(F32)).astype(BF16)
            first = pos * per_block
            ab[first:first + per_block, :rank, j * CHUNK:(j + 1) * CHUNK] = high
            ab[first:first + per_block, rank:, j * CHUNK:(j + 1) * CHUNK] = low
        for k in range(per_block):
            ga[...] += dot_nt(at[pos, k], at[pos, k])

    def peak_mode(first, count, copy):
        step = 2 if count % 2 == 0 else 1

        def body(i, carry):
            if copy is not None:
                for k in range(step):
                    copy(i * step + k).wait()
            total = acc[...]
            for k in range(step):
                index = first + i * step + k
                total += dot(ab[index], xbuf[index])
            acc[...] = total
            return carry

        lax.fori_loop(0, count // step, body, 0)

    def pair_peak(d, k):
        index = 2 * (d - 1) * per_block + k
        acc[...] += dot(ab[index], xbuf[index]) + dot(
            ab[index + per_block], xbuf[index + per_block]
        )

    def sib_send(chip_slot, k):
        pos = 2 * chip_slot
        return pltpu.make_async_remote_copy(
            src_ref=part.at[pos * per_block + k], dst_ref=sib.at[chip_slot, k],
            send_sem=s_ssem.at[chip_slot, k], recv_sem=s_rsem.at[chip_slot, k],
            device_id=(pix, sibling), device_id_type=MESH,
        )

    def far_send(d, k):
        device = 2 * lax.rem(chip + d, n_chip) + core
        pos = 2 * (d - 1) + 1
        return pltpu.make_async_remote_copy(
            src_ref=part.at[pos * per_block + k], dst_ref=far.at[d - 1, k],
            send_sem=f_ssem.at[d - 1, k], recv_sem=f_rsem.at[d - 1, k],
            device_id=(pix, device), device_id_type=MESH,
        )

    def pair_mode(d, k):
        index = 2 * (d - 1) * per_block + k
        pix_chunks([index, index + per_block])
        sib_send(d - 1, k).start()

    def pair_finish(d, k):
        sib_send(d - 1, k).wait_recv()
        part[(2 * (d - 1) + 1) * per_block + k] += sib[d - 1, k]
        far_send(d, k).start()

    acc[...] = jnp.zeros_like(acc)
    expand(own)

    pl.semaphore_wait(barrier, n_peak - 1 + n_pix - 1)

    def a_send(index, src, dst, device):
        return pltpu.make_async_remote_copy(
            src_ref=at.at[src], dst_ref=at.at[dst],
            send_sem=a_ssem.at[index], recv_sem=a_rsem.at[dst],
            device_id=(pix, device), device_id_type=MESH,
        )

    a_out = []
    for d in range(1, n_chip):
        device = 2 * lax.rem(chip - d + n_chip, n_chip) + core
        a_out.append(a_send(2 * (d - 1), own, 2 * (d - 1) + 1, device))
        a_out[-1].start()
    a_out.append(a_send(near, own, near, sibling))
    a_out[-1].start()
    a_fwd = [
        a_send(2 * (d - 1) + 1, 2 * (d - 1) + 1, 2 * (d - 1), sibling) for d in range(1, n_chip)
    ]

    g_out = []
    for d in range(1, n_peak):
        g_out.append(pltpu.make_async_remote_copy(
            src_ref=gc.at[0], dst_ref=gc.at[d],
            send_sem=g_ssem.at[d - 1], recv_sem=g_rsem.at[d - 1],
            device_id=(pix, lax.rem(me + d, n_peak)), device_id_type=MESH,
        ))
        g_out[-1].start()

    for p in first:
        for copy in pair_x(*p):
            copy.wait()
        pair_mode(*p)
    peak_mode(own * per_block, per_block, lambda k: x_copy(own, k))
    for copy in a_out:
        copy.wait_recv()
    for copy in a_fwd:
        copy.start()
    for p in first:
        pair_finish(*p)
    for p in second:
        for copy in pair_x(*p):
            copy.wait()
    expand(near)
    for p in second:
        pair_mode(*p)
    for copy in a_fwd:
        copy.wait_recv()
    for pos in range(near):
        expand(pos)
    for p in first + second:
        pair_peak(*p)
    for p in second:
        pair_finish(*p)
    acc[:rank, :] -= dot3(split3(ga[...] * gram_b), c_ref[...])
    peak_mode(near * per_block, per_block, lambda k: x_copy(near, k))
    for p in third + late:
        for copy in pair_x(*p):
            copy.wait()
        pair_peak(*p)

    pbuf[...] = ((acc[:rank, :] + acc[rank:, :]) * scale).reshape(pbuf.shape)
    r_out = []
    for d in range(1, n_pix):
        device = lax.rem(pix + d, n_pix)
        r_out.append(pltpu.make_async_remote_copy(
            src_ref=pbuf.at[device], dst_ref=rbuf.at[d - 1],
            send_sem=r_ssem.at[d - 1], recv_sem=r_rsem.at[d - 1],
            device_id=(device, me), device_id_type=MESH,
        ))
        r_out[-1].start()

    for n, p in enumerate(third + late):
        pair_mode(*p)
        if n > 0:
            pair_finish(*(third + late)[n - 1])

    def single_mode(pos, send, lo, hi):
        step = 2 if lo % 2 == 0 and hi % 2 == 0 else 1

        def body(i, carry):
            pix_chunks([pos * per_block + i * step + k for k in range(step)])
            if send:
                for k in range(step):
                    sib_send(n_chip - 1, i * step + k).start()
            return carry

        lax.fori_loop(lo // step, hi // step, body, 0)

    for d in range(1, n_peak):
        g_out[d - 1].wait_recv()
    gram_c = gc[0]
    for d in range(1, n_peak):
        gram_c += gc[d]
    weight = split3(gram_b * gram_c[:, :rank])
    for k in range(per_block):
        fix[k] = dot3(weight, at[own, k])
    for p in late[-1:]:
        pair_finish(*p)
    single_mode(near, True, 0, per_block // 2)

    for d in range(1, n_pix):
        r_out[d - 1].wait_recv()
    total = pbuf[pix]
    for d in range(1, n_pix):
        total += rbuf[d - 1]
    gpeak_ref[pix] = total
    o_out = []
    for d in range(1, n_pix):
        device = lax.rem(pix + d, n_pix)
        o_out.append(pltpu.make_async_remote_copy(
            src_ref=gpeak_ref.at[pix], dst_ref=gpeak_ref.at[pix],
            send_sem=o_ssem.at[d - 1], recv_sem=o_rsem.at[d - 1],
            device_id=(device, me), device_id_type=MESH,
        ))
        o_out[-1].start()

    single_mode(near, True, per_block // 2, per_block)
    single_mode(own, False, 0, per_block)

    for k in range(per_block):
        sib_send(n_chip - 1, k).wait_recv()
    for p in pairs:
        far_send(*p).wait_recv()
    for k in range(per_block):
        total = part[own * per_block + k] + sib[n_chip - 1, k]
        for d in range(1, n_chip):
            total += far[d - 1, k]
        total = total.T
        lo = k * CHUNK
        gpix_ref[:, lo:lo + half] = total[:rank] - fix[k, :, :half]
        gpix_ref[:, lo + half:lo + CHUNK] = total[rank:] - fix[k, :, half:]

    for d in range(1, n_pix):
        o_out[d - 1].wait_recv()
    for copy in a_out + a_fwd + g_out + r_out + o_out:
        copy.wait_send()
    for chip_slot in range(n_chip):
        for k in range(per_block):
            sib_send(chip_slot, k).wait_send()
    for p in pairs:
        far_send(*p).wait_send()


def place(pix_in, peak_in, pix_out, peak_out):
    pix_out[...] = pix_in[...]
    peak_out[...] = peak_in[...]


def solution(mesh):
    n_pix, n_peak = mesh.shape["pix"], mesh.shape["peak"]

    def on_device(cube, pix_factor, sec_factor, peak_factor):
        pixels, sections, peaks = cube.shape
        rank = peak_factor.shape[1]
        own = pix_factor.shape[0]
        per_block = own // CHUNK
        rows = CHUNK * sections
        n_chip = n_peak // 2
        n_far = max(n_chip - 1, 1)
        n_chunk = n_peak * per_block
        scale = 1.0 / math.sqrt(float(sections * pixels * n_pix))
        dma = pltpu.SemaphoreType.DMA
        vmem = pl.BlockSpec(memory_space=pltpu.VMEM)
        anywhere = pl.BlockSpec(memory_space=pl.ANY)
        packed = (CHUNK // 2, 2 * rank)
        grad_pix, grad_peak = pl.pallas_call(
            functools.partial(kernel, n_pix, n_peak, per_block, scale),
            out_shape=(
                jax.ShapeDtypeStruct((rank, own), F32),
                jax.ShapeDtypeStruct((n_pix, rank // n_pix, peaks), F32),
            ),
            in_specs=[anywhere, vmem, vmem, vmem],
            out_specs=(vmem, vmem),
            scratch_shapes=[
                pltpu.VMEM((n_chunk, rows, peaks), BF16),
                pltpu.VMEM((n_peak, per_block, rank, CHUNK), BF16),
                pltpu.VMEM((sections, CHUNK, CHUNK), BF16),
                pltpu.VMEM((n_chunk, 2 * rank, rows), BF16),
                pltpu.VMEM((n_chunk,) + packed, F32),
                pltpu.VMEM((n_chip, per_block) + packed, F32),
                pltpu.VMEM((n_far, per_block) + packed, F32),
                pltpu.VMEM((n_peak, rank, 2 * rank), F32),
                pltpu.VMEM((2 * rank, peaks), F32),
                pltpu.VMEM((n_pix, rank // n_pix, peaks), F32),
                pltpu.VMEM((n_pix - 1, rank // n_pix, peaks), F32),
                pltpu.VMEM((peaks, 2 * rank), BF16),
                pltpu.VMEM((rank, CHUNK), F32),
                pltpu.VMEM((rank, rank), F32),
                pltpu.VMEM((per_block, rank, CHUNK), F32),
                dma((n_chunk,)),
                dma((n_peak - 1,)), dma((n_peak - 1,)),
                dma((n_peak - 1,)), dma((n_peak - 1,)),
                dma((n_chip, per_block)), dma((n_chip, per_block)),
                dma((n_far, per_block)), dma((n_far, per_block)),
                dma((n_pix - 1,)), dma((n_pix - 1,)),
                dma((n_pix - 1,)), dma((n_pix - 1,)),
            ],
            compiler_params=pltpu.CompilerParams(
                collective_id=0, has_side_effects=True, vmem_limit_bytes=56 * 1024 * 1024
            ),
            name="cp_gradient",
        )(cube.reshape(pixels * sections, peaks), pix_factor.T, sec_factor, peak_factor.T)
        grad_pix, grad_peak = pl.pallas_call(
            place,
            out_shape=(
                jax.ShapeDtypeStruct((rank, own), F32),
                jax.ShapeDtypeStruct((rank, peaks), F32),
            ),
            in_specs=[vmem, vmem],
            out_specs=(vmem, vmem),
            name="place_results",
        )(grad_pix, grad_peak.reshape(rank, peaks))
        return grad_pix.T, grad_peak.T

    in_specs = (P("pix", None, "peak"), P(("pix", "peak"), None), P(), P("peak", None))
    out_specs = (P(("pix", "peak"), None), P("peak", None))
    return jax.shard_map(
        on_device, mesh=mesh, in_specs=in_specs, out_specs=out_specs, check_vma=False
    )
```

```python
import functools
import math

import jax
import jax.numpy as jnp
from jax import lax
from jax.experimental import pallas as pl
from jax.experimental.pallas import tpu as pltpu
from jax.sharding import PartitionSpec as P

MESH = pl.DeviceIdType.MESH
F32 = jnp.float32
BF16 = jnp.bfloat16
CHUNK = 256


def dot(a, b):
    return jnp.dot(a, b, preferred_element_type=F32)


def dot_nt(a, b):
    return lax.dot_general(a, b, (((1,), (1,)), ((), ())), preferred_element_type=F32)


def split3(x):
    one = x.astype(BF16)
    rest = x - one.astype(F32)
    two = rest.astype(BF16)
    return one, two, (rest - two.astype(F32)).astype(BF16)


def dot3(parts, b):
    return dot(parts[0], b) + (dot(parts[1], b) + dot(parts[2], b))


def kernel(
    n_pix, n_peak, per_block, scale,
    x_hbm, a_ref, b_ref, c_ref,
    gpix_ref, gpeak_ref,
    xbuf, at, spread, ab, part, sib, far, gc, acc, pbuf, rbuf, cc, bt, ga, fix,
    x_sem, a_ssem, a_rsem, g_ssem, g_rsem, s_ssem, s_rsem, f_ssem, f_rsem,
    r_ssem, r_rsem, o_ssem, o_rsem,
):
    rank = c_ref.shape[0]
    sections = b_ref.shape[0]
    rows = CHUNK * sections
    half = CHUNK // 2
    n_chip = n_peak // 2
    wide_r = 2 * rank
    pix = lax.axis_index("pix")
    me = lax.axis_index("peak")
    chip = me // 2
    core = lax.rem(me, 2)
    sibling = 2 * chip + 1 - core
    own = n_peak - 1
    near = n_peak - 2

    blocks = []
    for d in range(1, n_chip):
        other = lax.rem(chip + d, n_chip)
        blocks += [2 * other + 1 - core, 2 * other + core]
    blocks += [sibling, me]

    pairs = [(d, k) for k in range(per_block) for d in range(1, n_chip)]
    cuts = [len(pairs) * n // 4 for n in range(5)]
    first, second, third, late = [pairs[lo:hi] for lo, hi in zip(cuts, cuts[1:])]

    def x_copy(pos, k):
        first = (blocks[pos] * per_block + k) * rows
        return pltpu.make_async_copy(
            x_hbm.at[pl.ds(pl.multiple_of(first, rows), rows), :],
            xbuf.at[pos * per_block + k],
            x_sem.at[pos * per_block + k],
        )

    def pair_x(d, k):
        return [x_copy(2 * (d - 1), k), x_copy(2 * (d - 1) + 1, k)]

    order = [c for p in first for c in pair_x(*p)] + [x_copy(own, k) for k in range(per_block)]
    order += [c for p in second for c in pair_x(*p)] + [x_copy(near, k) for k in range(per_block)]
    order += [c for p in third + late for c in pair_x(*p)]
    for copy in order:
        copy.start()

    barrier = pltpu.get_barrier_semaphore()
    for d in range(1, n_peak):
        pl.semaphore_signal(
            barrier, inc=1, device_id=(pix, lax.rem(me + d, n_peak)), device_id_type=MESH
        )
    for d in range(1, n_pix):
        pl.semaphore_signal(
            barrier, inc=1, device_id=(lax.rem(pix + d, n_pix), me), device_id_type=MESH
        )

    for k in range(per_block):
        at[own, k] = a_ref[:, k * CHUNK:(k + 1) * CHUNK]
    ct = c_ref[...].astype(F32)
    cc[...] = jnp.concatenate([ct, ct], axis=0).T.astype(BF16)
    gc[0] = dot(c_ref[...], cc[...])

    row = lax.broadcasted_iota(jnp.int32, (rank, rank), 0)
    col = lax.broadcasted_iota(jnp.int32, (rank, rank), 1)
    eye = (row == col).astype(F32).astype(BF16)
    row = lax.broadcasted_iota(jnp.int32, (rank, wide_r), 0)
    col = lax.broadcasted_iota(jnp.int32, (rank, wide_r), 1)
    eye2 = ((row == col) | (row + rank == col)).astype(F32).astype(BF16)
    b_f = b_ref[...].astype(F32)
    b_tiled = jnp.broadcast_to(b_f[None], (CHUNK // sections, sections, rank))
    b_tiled = b_tiled.reshape(CHUNK, rank)
    bt[...] = dot_nt(eye, b_tiled.astype(BF16))
    bb = dot(b_ref[...], eye2)
    lead = lax.broadcasted_iota(jnp.int32, (CHUNK, rank), 0) < sections
    b_once = jnp.where(lead, b_tiled, 0.0).astype(BF16)
    gram_b = dot(dot_nt(eye, b_once).astype(BF16), b_once)
    row = lax.broadcasted_iota(jnp.int32, (CHUNK, CHUNK), 0)
    col = lax.broadcasted_iota(jnp.int32, (CHUNK, CHUNK), 1) // sections
    for j in range(sections):
        spread[j] = (row == col + j * (CHUNK // sections)).astype(F32).astype(BF16)
    ga[...] = jnp.zeros_like(ga)

    lane_lo = lax.broadcasted_iota(jnp.int32, (half * sections, wide_r), 1) < rank
    bb_all = jnp.broadcast_to(bb[None], (half, sections, wide_r))
    sub = lax.broadcasted_iota(jnp.int32, (half // sections, sections, wide_r), 1)

    def roll(x, shift):
        return pltpu.roll(x, shift % sections, 1)

    def section_sum(x):
        level = [x[:, n] for n in range(sections)]
        step = sections // 2
        while step >= 1:
            mask = lax.rem(sub, 2 * step) < step
            pairs_of = list(zip(level[:step], level[step:]))
            if 2 * step == sections:
                level = [
                    jnp.where(mask, one, two) + roll(jnp.where(mask, two, one), step)
                    for one, two in pairs_of
                ]
            else:
                level = [
                    jnp.where(mask, one + roll(one, -step), two + roll(two, step))
                    for one, two in pairs_of
                ]
            step //= 2
        return level[0]

    def pix_chunks(todo):
        for index in todo:
            full = dot(xbuf[index], cc[...])
            both = jnp.where(lane_lo, full[: half * sections], full[half * sections:])
            both = both.reshape(half, sections, wide_r) * bb_all
            both = both.reshape(half // sections, sections, sections, wide_r)
            part[index] = section_sum(both).reshape(half, wide_r)

    def expand(pos):
        stacked = at[pos].reshape(per_block * rank, CHUNK)
        for j in range(sections):
            product = dot(stacked, spread[j]).reshape(per_block, rank, CHUNK) * bt[...][None]
            high = product.astype(BF16)
            low = (product - high.astype(F32)).astype(BF16)
            first = pos * per_block
            ab[first:first + per_block, :rank, j * CHUNK:(j + 1) * CHUNK] = high
            ab[first:first + per_block, rank:, j * CHUNK:(j + 1) * CHUNK] = low
        for k in range(per_block):
            ga[...] += dot_nt(at[pos, k], at[pos, k])

    def peak_mode(first, count, copy):
        step = 2 if count % 2 == 0 else 1

        def body(i, carry):
            if copy is not None:
                for k in range(step):
                    copy(i * step + k).wait()
            total = acc[...]
            for k in range(step):
                index = first + i * step + k
                total += dot(ab[index], xbuf[index])
            acc[...] = total
            return carry

        lax.fori_loop(0, count // step, body, 0)

    def pair_peak(d, k):
        index = 2 * (d - 1) * per_block + k
        acc[...] += dot(ab[index], xbuf[index]) + dot(
            ab[index + per_block], xbuf[index + per_block]
        )

    def sib_send(chip_slot, k):
        pos = 2 * chip_slot
        return pltpu.make_async_remote_copy(
            src_ref=part.at[pos * per_block + k], dst_ref=sib.at[chip_slot, k],
            send_sem=s_ssem.at[chip_slot, k], recv_sem=s_rsem.at[chip_slot, k],
            device_id=(pix, sibling), device_id_type=MESH,
        )

    def far_send(d, k):
        device = 2 * lax.rem(chip + d, n_chip) + core
        pos = 2 * (d - 1) + 1
        return pltpu.make_async_remote_copy(
            src_ref=part.at[pos * per_block + k], dst_ref=far.at[d - 1, k],
            send_sem=f_ssem.at[d - 1, k], recv_sem=f_rsem.at[d - 1, k],
            device_id=(pix, device), device_id_type=MESH,
        )

    def pair_mode(d, k):
        index = 2 * (d - 1) * per_block + k
        pix_chunks([index, index + per_block])
        sib_send(d - 1, k).start()

    def pair_finish(d, k):
        sib_send(d - 1, k).wait_recv()
        part[(2 * (d - 1) + 1) * per_block + k] += sib[d - 1, k]
        far_send(d, k).start()

    acc[...] = jnp.zeros_like(acc)
    expand(own)

    pl.semaphore_wait(barrier, n_peak - 1 + n_pix - 1)

    def a_send(index, src, dst, device):
        return pltpu.make_async_remote_copy(
            src_ref=at.at[src], dst_ref=at.at[dst],
            send_sem=a_ssem.at[index], recv_sem=a_rsem.at[dst],
            device_id=(pix, device), device_id_type=MESH,
        )

    a_out = []
    for d in range(1, n_chip):
        device = 2 * lax.rem(chip - d + n_chip, n_chip) + core
        a_out.append(a_send(2 * (d - 1), own, 2 * (d - 1) + 1, device))
        a_out[-1].start()
    a_out.append(a_send(near, own, near, sibling))
    a_out[-1].start()
    a_fwd = [
        a_send(2 * (d - 1) + 1, 2 * (d - 1) + 1, 2 * (d - 1), sibling) for d in range(1, n_chip)
    ]

    g_out = []
    for d in range(1, n_peak):
        g_out.append(pltpu.make_async_remote_copy(
            src_ref=gc.at[0], dst_ref=gc.at[d],
            send_sem=g_ssem.at[d - 1], recv_sem=g_rsem.at[d - 1],
            device_id=(pix, lax.rem(me + d, n_peak)), device_id_type=MESH,
        ))
        g_out[-1].start()

    for p in first:
        for copy in pair_x(*p):
            copy.wait()
        pair_mode(*p)
    peak_mode(own * per_block, per_block, lambda k: x_copy(own, k))
    for copy in a_out:
        copy.wait_recv()
    for copy in a_fwd:
        copy.start()
    for p in first:
        pair_finish(*p)
    for p in second:
        for copy in pair_x(*p):
            copy.wait()
    expand(near)
    for p in second:
        pair_mode(*p)
    for copy in a_fwd:
        copy.wait_recv()
    for pos in range(near):
        expand(pos)
    for p in first + second:
        pair_peak(*p)
    for p in second:
        pair_finish(*p)
    acc[:rank, :] -= dot3(split3(ga[...] * gram_b), c_ref[...])
    peak_mode(near * per_block, per_block, lambda k: x_copy(near, k))
    for p in third + late:
        for copy in pair_x(*p):
            copy.wait()
        pair_peak(*p)

    pbuf[...] = ((acc[:rank, :] + acc[rank:, :]) * scale).reshape(pbuf.shape)
    r_out = []
    for d in range(1, n_pix):
        device = lax.rem(pix + d, n_pix)
        r_out.append(pltpu.make_async_remote_copy(
            src_ref=pbuf.at[device], dst_ref=rbuf.at[d - 1],
            send_sem=r_ssem.at[d - 1], recv_sem=r_rsem.at[d - 1],
            device_id=(device, me), device_id_type=MESH,
        ))
        r_out[-1].start()

    for n, p in enumerate(third + late):
        pair_mode(*p)
        if n > 0:
            pair_finish(*(third + late)[n - 1])

    def single_mode(pos, send, lo, hi):
        step = math.gcd(math.gcd(lo, hi), 4)

        def body(i, carry):
            pix_chunks([pos * per_block + i * step + k for k in range(step)])
            if send:
                for k in range(step):
                    sib_send(n_chip - 1, i * step + k).start()
            return carry

        lax.fori_loop(lo // step, hi // step, body, 0)

    for d in range(1, n_peak):
        g_out[d - 1].wait_recv()
    gram_c = gc[0]
    for d in range(1, n_peak):
        gram_c += gc[d]
    weight = split3(gram_b * gram_c[:, :rank])
    for k in range(per_block):
        fix[k] = dot3(weight, at[own, k])
    for p in late[-1:]:
        pair_finish(*p)
    single_mode(near, True, 0, per_block // 2)

    for d in range(1, n_pix):
        r_out[d - 1].wait_recv()
    total = pbuf[pix]
    for d in range(1, n_pix):
        total += rbuf[d - 1]
    gpeak_ref[pix] = total
    o_out = []
    for d in range(1, n_pix):
        device = lax.rem(pix + d, n_pix)
        o_out.append(pltpu.make_async_remote_copy(
            src_ref=gpeak_ref.at[pix], dst_ref=gpeak_ref.at[pix],
            send_sem=o_ssem.at[d - 1], recv_sem=o_rsem.at[d - 1],
            device_id=(device, me), device_id_type=MESH,
        ))
        o_out[-1].start()

    single_mode(near, True, per_block // 2, per_block)
    single_mode(own, False, 0, per_block)

    for k in range(per_block):
        sib_send(n_chip - 1, k).wait_recv()
    for p in pairs:
        far_send(*p).wait_recv()
    for k in range(per_block):
        total = part[own * per_block + k] + sib[n_chip - 1, k]
        for d in range(1, n_chip):
            total += far[d - 1, k]
        total = total.T
        lo = k * CHUNK
        gpix_ref[:, lo:lo + half] = total[:rank] - fix[k, :, :half]
        gpix_ref[:, lo + half:lo + CHUNK] = total[rank:] - fix[k, :, half:]

    for d in range(1, n_pix):
        o_out[d - 1].wait_recv()
    for copy in a_out + a_fwd + g_out + r_out + o_out:
        copy.wait_send()
    for chip_slot in range(n_chip):
        for k in range(per_block):
            sib_send(chip_slot, k).wait_send()
    for p in pairs:
        far_send(*p).wait_send()


def place(pix_in, peak_in, pix_out, peak_out):
    pix_out[...] = pix_in[...]
    peak_out[...] = peak_in[...]


def solution(mesh):
    n_pix, n_peak = mesh.shape["pix"], mesh.shape["peak"]

    def on_device(cube, pix_factor, sec_factor, peak_factor):
        pixels, sections, peaks = cube.shape
        rank = peak_factor.shape[1]
        own = pix_factor.shape[0]
        per_block = own // CHUNK
        rows = CHUNK * sections
        n_chip = n_peak // 2
        n_far = max(n_chip - 1, 1)
        n_chunk = n_peak * per_block
        scale = 1.0 / math.sqrt(float(sections * pixels * n_pix))
        dma = pltpu.SemaphoreType.DMA
        vmem = pl.BlockSpec(memory_space=pltpu.VMEM)
        anywhere = pl.BlockSpec(memory_space=pl.ANY)
        packed = (CHUNK // 2, 2 * rank)
        grad_pix, grad_peak = pl.pallas_call(
            functools.partial(kernel, n_pix, n_peak, per_block, scale),
            out_shape=(
                jax.ShapeDtypeStruct((rank, own), F32),
                jax.ShapeDtypeStruct((n_pix, rank // n_pix, peaks), F32),
            ),
            in_specs=[anywhere, vmem, vmem, vmem],
            out_specs=(vmem, vmem),
            scratch_shapes=[
                pltpu.VMEM((n_chunk, rows, peaks), BF16),
                pltpu.VMEM((n_peak, per_block, rank, CHUNK), BF16),
                pltpu.VMEM((sections, CHUNK, CHUNK), BF16),
                pltpu.VMEM((n_chunk, 2 * rank, rows), BF16),
                pltpu.VMEM((n_chunk,) + packed, F32),
                pltpu.VMEM((n_chip, per_block) + packed, F32),
                pltpu.VMEM((n_far, per_block) + packed, F32),
                pltpu.VMEM((n_peak, rank, 2 * rank), F32),
                pltpu.VMEM((2 * rank, peaks), F32),
                pltpu.VMEM((n_pix, rank // n_pix, peaks), F32),
                pltpu.VMEM((n_pix - 1, rank // n_pix, peaks), F32),
                pltpu.VMEM((peaks, 2 * rank), BF16),
                pltpu.VMEM((rank, CHUNK), F32),
                pltpu.VMEM((rank, rank), F32),
                pltpu.VMEM((per_block, rank, CHUNK), F32),
                dma((n_chunk,)),
                dma((n_peak - 1,)), dma((n_peak - 1,)),
                dma((n_peak - 1,)), dma((n_peak - 1,)),
                dma((n_chip, per_block)), dma((n_chip, per_block)),
                dma((n_far, per_block)), dma((n_far, per_block)),
                dma((n_pix - 1,)), dma((n_pix - 1,)),
                dma((n_pix - 1,)), dma((n_pix - 1,)),
            ],
            compiler_params=pltpu.CompilerParams(
                collective_id=0, has_side_effects=True, vmem_limit_bytes=56 * 1024 * 1024
            ),
            name="cp_gradient",
        )(cube.reshape(pixels * sections, peaks), pix_factor.T, sec_factor, peak_factor.T)
        grad_pix, grad_peak = pl.pallas_call(
            place,
            out_shape=(
                jax.ShapeDtypeStruct((rank, own), F32),
                jax.ShapeDtypeStruct((rank, peaks), F32),
            ),
            in_specs=[vmem, vmem],
            out_specs=(vmem, vmem),
            name="place_results",
        )(grad_pix, grad_peak.reshape(rank, peaks))
        return grad_pix.T, grad_peak.T

    in_specs = (P("pix", None, "peak"), P(("pix", "peak"), None), P(), P("peak", None))
    out_specs = (P(("pix", "peak"), None), P("peak", None))
    return jax.shard_map(
        on_device, mesh=mesh, in_specs=in_specs, out_specs=out_specs, check_vma=False
    )
```
